768 devices in a mesh: lat: 16 (over y_hi, x), lon: 48 (over z, y_lo, core).
Axes of the slice: x: 4, y: 8 (y_hi: 4, y_lo: 2; y = y_hi * 2 + y_lo), z: 12, core: 2. Of those that a mesh axis runs over, the one named last changes fastest.
Arguments:
- swath_input: bfloat16 [1536, 64, 64, 256], P(('lat', 'lon')), may hold values from -6 to 6
- conv_weight: bfloat16 [3, 3, 256, 256], replicated, may hold values from -0.125 to 0.125
- conv_bias: float32 [256], replicated, may hold values from -3 to 3
- block_band: int32 [1536, 1], P(('lat', 'lon')), may hold values from 0 to 15, as said below
- row_offset: int32 [1536], P(('lat', 'lon')), may hold values from 0 to 8
- col_offset: int32 [1536], P(('lat', 'lon')), may hold values from 0 to 8
- row_weights: bfloat16 [1536, 16, 32], P(('lat', 'lon')), may hold values from -1 to 1
- col_weights: bfloat16 [1536, 16, 32], P(('lat', 'lon')), may hold values from -1 to 1
- background: bfloat16 [384, 1152, 256], P('lat', 'lon'), may hold values from -6 to 6
- depth_weight: float32 [2, 7, 7, 256], replicated, may hold values from -0.875 to 0.875
- norm_gain: float32 [2, 256], replicated, may hold values from 0.1 to 1.9
- up_weight: bfloat16 [2, 256, 1024], replicated, may hold values from -0.375 to 0.375
- down_weight: bfloat16 [2, 1024, 256], replicated, may hold values from -0.1875 to 0.1875
Outputs:
- weather_grid: bfloat16 [384, 1152, 256], P('lat', 'lon')
The draws below stay inside these ranges and needn't reach their ends.
Inputs may be any that keep to these rules, and one draw needn't show every extreme that they name: `block_band`: block b's band is the latitude band (b // 2) // 48 of the device that holds it, or one next to it; every device sends at least one block to a neighbouring band, at most 2 to each, and some device sends exactly 2 to one.
All inputs are finite; a program needn't handle non-finite values.
Results may differ from the reference program's by a relative error of at most 0.011.
Values may be sent and summed in bfloat16 or wider, within the bound.
A program may use at most 64 MiB of HBM per device.

```python
import jax
import jax.numpy as jnp
from jax import lax

C = 256
HID = 1024
KS = 7
HALO = 3
LAYERS = 2
NB = 2
OBH = 32
OBW = 32
IBH = 64
IBW = 64
RB = 16
RW = 16
TH = 24
TW = 24
BANDS = 16
TILES_LON = 48
BLOCKS = 1536
GH = 384
GW = 1152
N_LON = 48


def draw_block_band(key, part):
    device_count = BLOCKS // NB
    device_ids = jnp.arange(device_count, dtype=jnp.int32)
    own_band = (device_ids // TILES_LON).astype(jnp.int32)
    key_side = jax.random.fold_in(key, 11)
    key_second = jax.random.fold_in(key, 23)
    side = (jax.random.randint(key_side, (device_count,), 0, 2).astype(jnp.int32) * 2 - 1).astype(jnp.int32)
    side = jnp.where(own_band == 0, 1, jnp.where(own_band == BANDS - 1, -1, side)).astype(jnp.int32)
    second = jax.random.randint(key_second, (device_count,), -1, 2).astype(jnp.int32)
    second = jnp.where(device_ids == 0, side, second).astype(jnp.int32)
    landing = own_band + second
    second = jnp.where((landing >= 0) & (landing < BANDS), second, 0).astype(jnp.int32)
    first_band = own_band + side
    second_band = own_band + second
    bands = jnp.stack([first_band, second_band], axis=1)
    return bands.reshape(BLOCKS, 1).astype(jnp.int32)


def plant(values, stream_key, smallest, high):
    place = [jax.random.randint(jax.random.fold_in(stream_key, axis), (), 0, length) for axis, length in enumerate(values.shape)]
    main_axis = values.shape.index(max(values.shape))
    beside = place[:main_axis] + [(place[main_axis] + 1) % values.shape[main_axis]] + place[main_axis + 1:]
    return values.at[tuple(place)].set(smallest).at[tuple(beside)].set(high)


def shard_levels(key, shape, shards, smallest, largest):
    level, own = 1.0, jax.random.fold_in(key, 6)
    for axis_at, blocks in shards:
        heights = jnp.exp(jax.random.uniform(jax.random.fold_in(own, axis_at), (blocks,), jnp.float32, smallest / len(shards), largest / len(shards)))
        level = level * jnp.repeat(heights, shape[axis_at] // blocks).reshape([-1 if axis == axis_at else 1 for axis in range(len(shape))])
    return level


def scatter_about(own_key, shape, deviation, bound, cuts=(), held_as=jnp.bfloat16):
    loudness = shard_levels(own_key, shape, cuts, -0.22, 0.18) if cuts else 1.0
    entries = jax.random.normal(own_key, shape, jnp.float32) * deviation * loudness
    return jnp.minimum(jnp.maximum(entries, -bound), bound).astype(held_as)


def setup_inputs(seed: int = 0) -> dict:
    seeds = jax.random.split(jax.random.key(seed), 14)
    return {
        "swath_input": scatter_about(seeds[0], (BLOCKS, IBH, IBW, C), 1.0, 6.0, ((0, 768),)),
        "conv_weight": scatter_about(seeds[1], (3, 3, C, C), (9 * C) ** -0.5, 0.125),
        "conv_bias": scatter_about(seeds[2], (C,), 0.5, 3.0, (), jnp.float32),
        "block_band": draw_block_band(jax.random.fold_in(seeds[13], 71), 0),
        "row_offset": plant(jax.random.randint(seeds[4], (BLOCKS,), 0, TH - RB + 1), jax.random.fold_in(seeds[4], 1), 0, TH - RB).astype(jnp.int32),
        "col_offset": plant(jax.random.randint(seeds[5], (BLOCKS,), 0, TW - RW + 1), jax.random.fold_in(seeds[5], 1), 0, TW - RW).astype(jnp.int32),
        "row_weights": scatter_about(seeds[6], (BLOCKS, RB, OBH), OBH ** -0.5, 1.0, ((0, 768),)),
        "col_weights": scatter_about(seeds[7], (BLOCKS, RW, OBW), OBW ** -0.5, 1.0, ((0, 768),)),
        "background": scatter_about(seeds[8], (GH, GW, C), 1.0, 6.0, ((0, 16), (1, 48))),
        "depth_weight": scatter_about(seeds[9], (LAYERS, KS, KS, C), (KS * KS) ** -0.5, 0.875, (), jnp.float32),
        "norm_gain": jnp.clip(1.0 + 0.18 * jax.random.normal(seeds[10], (LAYERS, C), jnp.float32), 0.1, 1.9),
        "up_weight": scatter_about(seeds[11], (LAYERS, C, HID), C ** -0.5, 0.375),
        "down_weight": scatter_about(seeds[12], (LAYERS, HID, C), HID ** -0.5, 0.1875),
    }


def resample_group(swath_group, conv_weight, conv_bias, row_group, col_group):
    convolved = lax.conv_general_dilated(swath_group.astype(jnp.float32), conv_weight.astype(jnp.float32), (2, 2), ((1, 1), (1, 1)), dimension_numbers=('NHWC', 'HWIO', 'NHWC'), precision=lax.Precision.HIGHEST)
    features = jax.nn.gelu(convolved + conv_bias).astype(jnp.bfloat16)
    row_mixed = jnp.einsum('nri,nijc->nrjc', row_group.astype(jnp.float32), features.astype(jnp.float32), precision=lax.Precision.HIGHEST)
    both_mixed = jnp.einsum('nrjc,nuj->nruc', row_mixed, col_group.astype(jnp.float32), precision=lax.Precision.HIGHEST)
    return both_mixed.astype(jnp.bfloat16)

def layer_apply(padded, depth_kernel, gain, up_matrix, down_matrix):
    height = padded.shape[0] - (KS - 1)
    width = padded.shape[1] - (KS - 1)
    channels = padded.shape[2]
    widened = padded.astype(jnp.float32)
    kernel = depth_kernel.reshape(KS, KS, 1, channels).astype(jnp.float32)
    mixed = lax.conv_general_dilated(widened[None], kernel, (1, 1), ((0, 0), (0, 0)), dimension_numbers=('NHWC', 'HWIO', 'NHWC'), feature_group_count=channels, precision=lax.Precision.HIGHEST)[0]
    centered = mixed - lax.optimization_barrier(jnp.mean(mixed, axis=-1, keepdims=True))
    variance = lax.optimization_barrier(jnp.mean(centered * centered, axis=-1, keepdims=True))
    normed = (centered * lax.rsqrt(variance + 1e-06) * gain).astype(jnp.bfloat16)
    flat_cells = normed.reshape(height * width, -1)
    hidden = jax.nn.gelu(jnp.dot(flat_cells, up_matrix, preferred_element_type=jnp.float32)).astype(jnp.bfloat16)
    output = jnp.dot(hidden, down_matrix, preferred_element_type=jnp.float32).reshape(height, width, -1)
    residual_part = widened[HALO:HALO + height, HALO:HALO + width]
    return (residual_part + output).astype(jnp.bfloat16)

def reference(swath_input, conv_weight, conv_bias, block_band, row_offset, col_offset, row_weights, col_weights, background, depth_weight, norm_gain, up_weight, down_weight):
    group_count = BLOCKS // NB
    swath_groups = swath_input.reshape(group_count, NB, IBH, IBW, C)
    row_groups = row_weights.reshape(group_count, NB, RB, OBH)
    col_groups = col_weights.reshape(group_count, NB, RW, OBW)
    resampled = lax.map(lambda packed: resample_group(packed[0], conv_weight, conv_bias, packed[1], packed[2]), (swath_groups, row_groups, col_groups))
    resampled = resampled.reshape(BLOCKS, RB, RW, C)
    block_index = jnp.arange(BLOCKS, dtype=jnp.int32)
    lon_tile = (block_index // NB % N_LON).astype(jnp.int32)
    row_start = (block_band[:, 0] * TH + row_offset).astype(jnp.int32)
    col_start = (lon_tile * TW + col_offset).astype(jnp.int32)

    def add_block(index, total):
        piece = resampled[index].astype(total.dtype)
        anchor = (row_start[index].astype(jnp.int32), col_start[index].astype(jnp.int32), jnp.zeros((), jnp.int32))
        current = lax.dynamic_slice(total, anchor, (RB, RW, C))
        return lax.dynamic_update_slice(total, current + piece, anchor)
    summed = lax.fori_loop(0, BLOCKS, add_block, jnp.zeros((GH, GW, C), jnp.float32))
    state = (background.astype(jnp.float32) + summed).astype(jnp.bfloat16)
    for layer_index in range(LAYERS):
        padded = jnp.pad(state, ((HALO, HALO), (0, 0), (0, 0)))
        padded = jnp.concatenate([padded[:, GW - HALO:], padded, padded[:, :HALO]], axis=1)
        state = layer_apply(padded, depth_weight[layer_index], norm_gain[layer_index], up_weight[layer_index], down_weight[layer_index])
    return state
```

```python
import functools

import jax
import jax.numpy as jnp
import numpy as np
from jax import lax
from jax.experimental import pallas as pl
from jax.experimental.pallas import tpu as pltpu
from jax.sharding import PartitionSpec as P

KS = 7
HALO = 3
LAYERS = 2
NB = 2
OB = 32
IB = 64
RB = 16
T = 24
CELLS = T * T
C = 256
HID = 1024
STRIP = 112
F32 = jnp.float32
BF16 = jnp.bfloat16
MESH = pl.DeviceIdType.MESH
DIAGS = ((1, 0), (-1, 0), (0, 1), (0, -1), (1, 1), (-1, 1), (1, -1), (-1, -1))


def strip_source(first_col):
    cells = np.full((STRIP,), -1)
    for k in range(9):
        cells[k] = (T - HALO + k // 3) * T + first_col + k % 3
        cells[96 + k] = (k // 3) * T + first_col + k % 3
    for k in range(3 * T):
        cells[16 + k] = (k // 3) * T + first_col + k % 3
    return cells


def pick_matrix(first_col):
    return (strip_source(first_col)[:, None] == np.arange(CELLS)[None, :]).astype(np.float32)


def spread_matrix(first):
    out = np.zeros((30 * 8, STRIP), np.float32)
    for y in range(30):
        base = y * 3 if y < 3 else (16 + (y - 3) * 3 if y < 27 else 96 + (y - 27) * 3)
        for t in range(3):
            out[y * 8 + first + t, base + t] = 1
    return out


def gelu(x):
    inner = x * (0.7978845608028654 + 0.035677408136300125 * (x * x))
    half = 0.5 * x
    return half + half * jnp.tanh(inner)


def body(
    nlat, nlon,
    band, roff, coff, swath, wconv, bias, roww, colw, back, depth, gain, up, down,
    pick_l, pick_r, spread_l, spread_r,
    out,
    x_s, w_s, up_s, dn_s, t_s, x3_s, feat_s, kron_s, own_s, north_s, south_s,
    meta_s, meta_n, meta_d, onehot_s, acc_s, st_s, pad_s, mix_s,
    edge_l, edge_r, strip_l, strip_r, top_s, bot_s,
    load_sem, bsend, brecv, msend, mrecv, hsend, hrecv,
):
    lat, lon = lax.axis_index("lat"), lax.axis_index("lon")

    def at(dlat, dlon):
        return (lax.rem(lat + dlat + nlat, nlat), lax.rem(lon + dlon + nlon, nlon))

    barrier = pltpu.get_barrier_semaphore()
    for d in DIAGS:
        pl.semaphore_signal(barrier, inc=1, device_id=at(*d), device_id_type=MESH)

    loads = [
        pltpu.make_async_copy(swath.at[0], x_s.at[0], load_sem.at[0]),
        pltpu.make_async_copy(wconv, w_s, load_sem.at[2]),
        pltpu.make_async_copy(swath.at[1], x_s.at[1], load_sem.at[1]),
        pltpu.make_async_copy(up, up_s, load_sem.at[3]),
        pltpu.make_async_copy(down, dn_s, load_sem.at[4]),
    ]
    for cp in loads:
        cp.start()

    row8 = lax.broadcasted_iota(jnp.int32, (8, C), 0)

    def codes(target):
        c0 = jnp.where(band[0, 0] == target, roff[0] * 64 + coff[0], -4096)
        c1 = jnp.where(band[1, 0] == target, roff[1] * 64 + coff[1], -4096)
        return jnp.where(row8 == 0, c0, jnp.where(row8 == 1, c1, -4096))

    meta_s[0] = codes(lat)
    meta_s[1] = codes(lat - 1)
    meta_s[2] = codes(lat + 1)

    cell = lax.broadcasted_iota(jnp.int32, (CELLS, C), 0)
    pos = lax.broadcasted_iota(jnp.int32, (CELLS, C), 1)
    h = (cell * 2731) >> 16
    w = cell - h * T
    diff = (h - (pos >> 4)) * 64 + (w - (pos & 15))
    acc_s[...] = diff

    def build_onehot(slot, meta_ref):
        for s in range(NB):
            code = meta_ref[s:s + 1, :]
            onehot_s[2 * slot + s] = jnp.where(acc_s[...] == code, 1.0, 0.0).astype(BF16)

    build_onehot(0, meta_s.at[0])

    m_i = lax.broadcasted_iota(jnp.int32, (RB * RB, RB), 0)
    r_i = lax.broadcasted_iota(jnp.int32, (RB * RB, RB), 1)
    exp_r = jnp.where((m_i >> 4) == r_i, 1.0, 0.0).astype(BF16)
    exp_u = jnp.where((m_i & 15) == r_i, 1.0, 0.0).astype(BF16)
    k_i = lax.broadcasted_iota(jnp.int32, (OB, OB * OB), 1)
    i_i = lax.broadcasted_iota(jnp.int32, (OB, OB * OB), 0)
    exp_i = jnp.where((k_i >> 5) == i_i, 1.0, 0.0).astype(BF16)
    exp_j = jnp.where((k_i & 31) == i_i, 1.0, 0.0).astype(BF16)
    for b in range(NB):
        rows = jnp.dot(exp_r, roww[b], preferred_element_type=F32).astype(BF16)
        cols = jnp.dot(exp_u, colw[b], preferred_element_type=F32).astype(BF16)
        for q in range(4):
            part = slice(q * 256, (q + 1) * 256)
            left = jnp.dot(rows, exp_i[:, part], preferred_element_type=F32)
            right = jnp.dot(cols, exp_j[:, part], preferred_element_type=F32)
            kron_s[b, :, part] = (left * right).astype(BF16)

    t_s[:, :, 0:8, :] = jnp.zeros((2, 8, 8, 128), F32)
    x3_s[0, 0] = jnp.zeros((OB, 3 * C), BF16)

    pl.semaphore_wait(barrier, len(DIAGS))
    metas = [
        pltpu.make_async_remote_copy(meta_s.at[1], meta_d, msend.at[0], mrecv.at[0], device_id=at(-1, 0), device_id_type=MESH),
        pltpu.make_async_remote_copy(meta_s.at[2], meta_n, msend.at[1], mrecv.at[1], device_id=at(1, 0), device_id_type=MESH),
    ]
    for cp in metas:
        cp.start()

    sends = []
    for b in range(NB):
        loads[0 if b == 0 else 2].wait()
        if b == 0:
            loads[1].wait()

        def spread_rows(g, _, b=b):
            for k in range(8):
                r = g * 8 + k
                for c in range(2):
                    t_s[c, k, 8:72, :] = x_s[b, r, :, c * 128:(c + 1) * 128].astype(F32)
            for k in range(8):
                hi, lo = (k + 1) // 2, (k + 1) % 2
                for e in range(3):
                    for c in range(2):
                        piece = t_s[c, k, pl.ds(7 + e, OB, stride=2), :].astype(BF16)
                        x3_s[g * 4 + hi, lo, :, e * C + c * 128:e * C + (c + 1) * 128] = piece
            return 0

        lax.fori_loop(0, 8, spread_rows, 0)

        def conv_rows(g, _):
            i0 = g * 8
            total = jnp.dot(x3_s[pl.ds(i0, 8), 0].reshape(256, 3 * C), w_s[0], preferred_element_type=F32)
            total += jnp.dot(x3_s[pl.ds(i0, 8), 1].reshape(256, 3 * C), w_s[1], preferred_element_type=F32)
            total += jnp.dot(x3_s[pl.ds(i0 + 1, 8), 0].reshape(256, 3 * C), w_s[2], preferred_element_type=F32)
            feat_s[pl.ds(pl.multiple_of(g * 256, 256), 256), :] = gelu(total + bias[...]).astype(BF16)
            return 0

        lax.fori_loop(0, 4, conv_rows, 0)
        own_s[b] = jnp.dot(kron_s[b], feat_s[...], preferred_element_type=F32).astype(BF16)
        pair = [
            pltpu.make_async_remote_copy(own_s.at[b], south_s.at[b], bsend.at[b, 0], brecv.at[b, 0], device_id=at(-1, 0), device_id_type=MESH),
            pltpu.make_async_remote_copy(own_s.at[b], north_s.at[b], bsend.at[b, 1], brecv.at[b, 1], device_id=at(1, 0), device_id_type=MESH),
        ]
        for cp in pair:
            cp.start()
        sends.append(pair)

    for cp in metas:
        cp.wait()
    build_onehot(1, meta_n)
    build_onehot(2, meta_d)

    for b in range(NB):
        for cp in sends[b]:
            cp.wait()
    for q in range(3):
        part = slice(q * 192, (q + 1) * 192)
        total = back[part, :].astype(F32)
        for b in range(NB):
            total += jnp.dot(onehot_s[b, part, :], own_s[b], preferred_element_type=F32)
            total += jnp.dot(onehot_s[2 + b, part, :], north_s[b], preferred_element_type=F32)
            total += jnp.dot(onehot_s[4 + b, part, :], south_s[b], preferred_element_type=F32)
        st_s[0, part, :] = total.astype(BF16)

    loads[3].wait()
    loads[4].wait()

    has_top = jnp.where(lat > 0, 1.0, 0.0).astype(F32)
    has_bot = jnp.where(lat < nlat - 1, 1.0, 0.0).astype(F32)

    for l in range(LAYERS):
        st = st_s.at[l]
        edge_l[l] = jnp.dot(pick_l[...], st[...], preferred_element_type=F32).astype(BF16)
        edge_r[l] = jnp.dot(pick_r[...], st[...], preferred_element_type=F32).astype(BF16)
        moves = [
            (st.at[pl.ds(496, 80)], bot_dst(top_s, l), (1, 0)),
            (st.at[pl.ds(0, 80)], bot_dst(bot_s, l), (-1, 0)),
            (edge_r.at[l, pl.ds(16, 80)], strip_l.at[l, pl.ds(16, 80)], (0, 1)),
            (edge_l.at[l, pl.ds(16, 80)], strip_r.at[l, pl.ds(16, 80)], (0, -1)),
            (edge_r.at[l, pl.ds(0, 16)], strip_l.at[l, pl.ds(0, 16)], (1, 1)),
            (edge_r.at[l, pl.ds(96, 16)], strip_l.at[l, pl.ds(96, 16)], (-1, 1)),
            (edge_l.at[l, pl.ds(0, 16)], strip_r.at[l, pl.ds(0, 16)], (1, -1)),
            (edge_l.at[l, pl.ds(96, 16)], strip_r.at[l, pl.ds(96, 16)], (-1, -1)),
        ]
        copies = [
            pltpu.make_async_remote_copy(src, dst, hsend.at[l, n], hrecv.at[l, n], device_id=at(*d), device_id_type=MESH)
            for n, (src, dst, d) in enumerate(moves)
        ]
        for cp in copies:
            cp.start()
        for c in range(2):
            lanes = slice(c * 128, (c + 1) * 128)
            pad_s[c, 3:27, 8:32, :] = st[:, lanes].astype(F32).reshape(T, T, 128)
        for cp in copies:
            cp.wait()
        left = jnp.dot(spread_l[...], strip_l[l], preferred_element_type=F32).reshape(30, 8, C)
        right = jnp.dot(spread_r[...], strip_r[l], preferred_element_type=F32).reshape(30, 8, C)
        upper = top_s[l].astype(F32)[8:80].reshape(3, T, C) * has_top
        lower = bot_s[l].astype(F32)[0:72].reshape(3, T, C) * has_bot
        for c in range(2):
            lanes = slice(c * 128, (c + 1) * 128)
            for side, lo in ((left, 0), (right, 32)):
                pad_s[c, 0:3, lo:lo + 8, :] = side[0:3, :, lanes] * has_top
                pad_s[c, 3:27, lo:lo + 8, :] = side[3:27, :, lanes]
                pad_s[c, 27:30, lo:lo + 8, :] = side[27:30, :, lanes] * has_bot
            pad_s[c, 0:3, 8:32, :] = upper[:, :, lanes]
            pad_s[c, 27:30, 8:32, :] = lower[:, :, lanes]

        def mix_rows(g, _, l=l):
            c, h0 = g // 3, (g % 3) * 8
            acc = [None] * 8
            for e in range(KS):
                wt = [depth[l, a, e, pl.ds(c, 1), :] for a in range(KS)]
                for r in range(14):
                    line = pad_s[c, h0 + r, 5 + e:29 + e, :]
                    for a in range(KS):
                        o = r - a
                        if 0 <= o < 8:
                            term = line * wt[a]
                            acc[o] = term if acc[o] is None else acc[o] + term
            for o in range(8):
                mix_s[c, h0 + o] = acc[o]
            return 0

        lax.fori_loop(0, 6, mix_rows, 0)

        def cells_step(g, _, l=l, st=st):
            m0 = mix_s[0, pl.ds(g * 8, 8)].reshape(192, 128)
            m1 = mix_s[1, pl.ds(g * 8, 8)].reshape(192, 128)
            mean = jnp.sum(m0 + m1, axis=-1, keepdims=True) * (1.0 / C)
            c0, c1 = m0 - mean, m1 - mean
            var = jnp.sum(c0 * c0 + c1 * c1, axis=-1, keepdims=True) * (1.0 / C)
            inv = lax.rsqrt(var + 1e-6)
            normed = jnp.concatenate(
                [(c0 * inv * gain[l:l + 1, 0:128]).astype(BF16), (c1 * inv * gain[l:l + 1, 128:256]).astype(BF16)], axis=1
            )
            hid = gelu(jnp.dot(normed, up_s[l], preferred_element_type=F32)).astype(BF16)
            part = pl.ds(pl.multiple_of(g * 192, 192), 192)
            new = st[part, :].astype(F32) + jnp.dot(hid, dn_s[l], preferred_element_type=F32)
            if l == LAYERS - 1:
                out[part, :] = new.astype(BF16)
            else:
                st_s[l + 1, part, :] = new.astype(BF16)
            return 0

        lax.fori_loop(0, 3, cells_step, 0)


def bot_dst(ref, l):
    return ref.at[l]


def solution(mesh):
    nlat, nlon = mesh.shape["lat"], mesh.shape["lon"]

    def per_device(swath, wconv, bias, band, roff, coff, roww, colw, back, depth, gain, up, down):
        smem = pl.BlockSpec(memory_space=pltpu.SMEM)
        vmem = pl.BlockSpec(memory_space=pltpu.VMEM)
        hbm = pl.BlockSpec(memory_space=pl.ANY)
        dma = pltpu.SemaphoreType.DMA
        result = pl.pallas_call(
            functools.partial(body, nlat, nlon),
            out_shape=jax.ShapeDtypeStruct((CELLS, C), BF16),
            in_specs=[smem, smem, smem, hbm, hbm] + [vmem] * 6 + [hbm, hbm] + [vmem] * 4,
            out_specs=vmem,
            scratch_shapes=[
                pltpu.VMEM((NB, IB, IB, C), BF16),
                pltpu.VMEM((3, 3 * C, C), BF16),
                pltpu.VMEM((LAYERS, C, HID), BF16),
                pltpu.VMEM((LAYERS, HID, C), BF16),
                pltpu.VMEM((2, 8, 72, 128), F32),
                pltpu.VMEM((33, 2, OB, 3 * C), BF16),
                pltpu.VMEM((OB * OB, C), BF16),
                pltpu.VMEM((NB, RB * RB, OB * OB), BF16),
                pltpu.VMEM((NB, RB * RB, C), BF16),
                pltpu.VMEM((NB, RB * RB, C), BF16),
                pltpu.VMEM((NB, RB * RB, C), BF16),
                pltpu.VMEM((3, 8, C), jnp.int32),
                pltpu.VMEM((8, C), jnp.int32),
                pltpu.VMEM((8, C), jnp.int32),
                pltpu.VMEM((3 * NB, CELLS, RB * RB), BF16),
                pltpu.VMEM((CELLS, C), jnp.int32),
                pltpu.VMEM((LAYERS, CELLS, C), BF16),
                pltpu.VMEM((2, 30, 40, 128), F32),
                pltpu.VMEM((2, T, T, 128), F32),
                pltpu.VMEM((LAYERS, STRIP, C), BF16),
                pltpu.VMEM((LAYERS, STRIP, C), BF16),
                pltpu.VMEM((LAYERS, STRIP, C), BF16),
                pltpu.VMEM((LAYERS, STRIP, C), BF16),
                pltpu.VMEM((LAYERS, 80, C), BF16),
                pltpu.VMEM((LAYERS, 80, C), BF16),
                dma((5,)),
                dma((NB, 2)),
                dma((NB, 2)),
                dma((2,)),
                dma((2,)),
                dma((LAYERS, 8)),
                dma((LAYERS, 8)),
            ],
            compiler_params=pltpu.CompilerParams(
                collective_id=0, has_side_effects=True, vmem_limit_bytes=56 * 1024 * 1024
            ),
        )(
            band, roff, coff, swath, wconv.reshape(3, 3 * C, C), bias.reshape(1, C), roww, colw,
            back.reshape(CELLS, C), depth.reshape(LAYERS, KS, KS, 2, 128), gain, up, down,
            jnp.asarray(pick_matrix(0), BF16), jnp.asarray(pick_matrix(T - HALO), BF16),
            jnp.asarray(spread_matrix(5), BF16), jnp.asarray(spread_matrix(0), BF16),
        )
        return result.reshape(T, T, C)

    split = P(("lat", "lon"))
    in_specs = (split, P(), P(), split, split, split, split, split, P("lat", "lon"), P(), P(), P(), P())
    return jax.shard_map(
        per_device, mesh=mesh, in_specs=in_specs, out_specs=P("lat", "lon", None), check_vma=False
    )
```

```python
import functools

import jax
import jax.numpy as jnp
import numpy as np
from jax import lax
from jax.experimental import pallas as pl
from jax.experimental.pallas import tpu as pltpu
from jax.sharding import PartitionSpec as P

KS = 7
HALO = 3
LAYERS = 2
NB = 2
OB = 32
IB = 64
RB = 16
T = 24
CELLS = T * T
C = 256
HID = 1024
SLOTS = 2
STRIP = 112
F32 = jnp.float32
BF16 = jnp.bfloat16
MESH = pl.DeviceIdType.MESH
DIAGS = ((1, 0), (-1, 0), (0, 1), (0, -1), (1, 1), (-1, 1), (1, -1), (-1, -1))


def strip_source(first_col):
    cells = np.full((STRIP,), -1)
    for k in range(9):
        cells[k] = (T - HALO + k // 3) * T + first_col + k % 3
        cells[96 + k] = (k // 3) * T + first_col + k % 3
    for k in range(3 * T):
        cells[16 + k] = (k // 3) * T + first_col + k % 3
    return cells


def pick_matrix(first_col):
    return (strip_source(first_col)[:, None] == np.arange(CELLS)[None, :]).astype(np.float32)


def spread_matrix(first):
    out = np.zeros((30 * 8, STRIP), np.float32)
    for y in range(30):
        base = y * 3 if y < 3 else (16 + (y - 3) * 3 if y < 27 else 96 + (y - 27) * 3)
        for t in range(3):
            out[y * 8 + first + t, base + t] = 1
    return out


def gelu(x):
    inner = x * (0.7978845608028654 + 0.035677408136300125 * (x * x))
    half = 0.5 * x
    return half + half * jnp.tanh(inner)


def body(
    nlat, nlon,
    band, roff, coff, swath, wconv, bias, roww, colw, back, depth, gain, up, down,
    pick_l, pick_r, spread_l, spread_r,
    out,
    x_s, w_s, up_s, dn_s, t_s, x3_s, feat_s, kron_s, own_s, north_s, south_s,
    meta_s, meta_n, meta_d, onehot_s, acc_s, sum_s, st_s, pad_s, mix_s,
    edge_l, edge_r, strip_l, strip_r, top_s, bot_s,
    roww_s, colw_s, bias_s, back_s, pick_ls, pick_rs, spread_ls, spread_rs, dep_s, gain_s,
    load_sem, bsend, brecv, msend, mrecv, hsend, hrecv,
):
    lat, lon = lax.axis_index("lat"), lax.axis_index("lon")

    def at(dlat, dlon):
        return (lax.rem(lat + dlat + nlat, nlat), lax.rem(lon + dlon + nlon, nlon))

    barrier = pltpu.get_barrier_semaphore()
    for d in DIAGS:
        pl.semaphore_signal(barrier, inc=1, device_id=at(*d), device_id_type=MESH)

    loads = [
        pltpu.make_async_copy(src, dst, load_sem.at[n])
        for n, (src, dst) in enumerate((
            (roww, roww_s), (colw, colw_s), (swath.at[0], x_s.at[0]), (bias, bias_s), (wconv, w_s), (swath.at[1], x_s.at[1]),
            (back, back_s), (pick_l, pick_ls), (pick_r, pick_rs), (spread_l, spread_ls), (spread_r, spread_rs),
            (depth, dep_s), (gain, gain_s), (up, up_s), (down, dn_s),
        ))
    ]
    for cp in loads:
        cp.start()

    row8 = lax.broadcasted_iota(jnp.int32, (8, C), 0)

    def codes(target):
        c0 = jnp.where(band[0] == target, roff[0] * 64 + coff[0], -4096)
        c1 = jnp.where(band[1] == target, roff[1] * 64 + coff[1], -4096)
        return jnp.where(row8 == 0, c0, jnp.where(row8 == 1, c1, -4096))

    meta_s[0] = codes(lat)
    meta_s[1] = codes(lat - 1)
    meta_s[2] = codes(lat + 1)

    cell = lax.broadcasted_iota(jnp.int32, (CELLS, C), 0)
    pos = lax.broadcasted_iota(jnp.int32, (CELLS, C), 1)
    h = (cell * 2731) >> 16
    w = cell - h * T
    diff = (h - (pos >> 4)) * 64 + (w - (pos & 15))
    acc_s[...] = diff

    def build_onehot(slot, meta_ref):
        for s in range(NB):
            code = meta_ref[s:s + 1, :]
            onehot_s[2 * slot + s] = jnp.where(acc_s[...] == code, 1.0, 0.0).astype(BF16)

    build_onehot(0, meta_s.at[0])

    m_i = lax.broadcasted_iota(jnp.int32, (RB * RB, RB), 0)
    r_i = lax.broadcasted_iota(jnp.int32, (RB * RB, RB), 1)
    exp_r = jnp.where((m_i >> 4) == r_i, 1.0, 0.0).astype(BF16)
    exp_u = jnp.where((m_i & 15) == r_i, 1.0, 0.0).astype(BF16)
    k_i = lax.broadcasted_iota(jnp.int32, (OB, OB * OB), 1)
    i_i = lax.broadcasted_iota(jnp.int32, (OB, OB * OB), 0)
    exp_i = jnp.where((k_i >> 5) == i_i, 1.0, 0.0).astype(BF16)
    exp_j = jnp.where((k_i & 31) == i_i, 1.0, 0.0).astype(BF16)
    loads[0].wait()
    loads[1].wait()
    for b in range(NB):
        rows = jnp.dot(exp_r, roww_s[b], preferred_element_type=F32).astype(BF16)
        cols = jnp.dot(exp_u, colw_s[b], preferred_element_type=F32).astype(BF16)
        for q in range(4):
            part = slice(q * 256, (q + 1) * 256)
            left = jnp.dot(rows, exp_i[:, part], preferred_element_type=F32)
            right = jnp.dot(cols, exp_j[:, part], preferred_element_type=F32)
            kron_s[b, :, part] = (left * right).astype(BF16)

    t_s[:, :, :, 0:8, :] = jnp.zeros((SLOTS, 2, 8, 8, 128), F32)
    x3_s[0, 0] = jnp.zeros((OB, 3 * C), BF16)

    sends = []
    for b in range(NB):
        loads[2 if b == 0 else 5].wait()
        if b == 0:
            loads[3].wait()
            loads[4].wait()

        def spread_rows(g, b=b):
            slot = g % SLOTS
            for k in range(8):
                for c in range(2):
                    t_s[slot, c, k, 8:72, :] = x_s[b, g * 8 + k, :, c * 128:(c + 1) * 128].astype(F32)
            for k in range(8):
                hi, lo = (k + 1) // 2, (k + 1) % 2
                for e in range(3):
                    for c in range(2):
                        piece = t_s[slot, c, k, pl.ds(7 + e, OB, stride=2), :].astype(BF16)
                        x3_s[g * 4 + hi, lo, :, e * C + c * 128:e * C + (c + 1) * 128] = piece

        def conv_rows(g):
            i0 = g * 8
            total = jnp.dot(x3_s[i0:i0 + 8, 0].reshape(256, 3 * C), w_s[0], preferred_element_type=F32)
            total += jnp.dot(x3_s[i0:i0 + 8, 1].reshape(256, 3 * C), w_s[1], preferred_element_type=F32)
            total += jnp.dot(x3_s[i0 + 1:i0 + 9, 0].reshape(256, 3 * C), w_s[2], preferred_element_type=F32)
            feat_s[g * 256:(g + 1) * 256, :] = gelu(total + bias_s[...]).astype(BF16)

        spread_rows(0)
        spread_rows(1)
        for g in range(4):
            if g < 3:
                spread_rows(2 * g + 2)
                spread_rows(2 * g + 3)
            conv_rows(g)
        own_s[b] = jnp.dot(kron_s[b], feat_s[...], preferred_element_type=F32).astype(BF16)
        if b == 0:
            pl.semaphore_wait(barrier, len(DIAGS))
            metas = [
                pltpu.make_async_remote_copy(meta_s.at[1], meta_d, msend.at[0], mrecv.at[0], device_id=at(-1, 0), device_id_type=MESH),
                pltpu.make_async_remote_copy(meta_s.at[2], meta_n, msend.at[1], mrecv.at[1], device_id=at(1, 0), device_id_type=MESH),
            ]
            for cp in metas:
                cp.start()
        pair = [
            pltpu.make_async_remote_copy(own_s.at[b], south_s.at[b], bsend.at[b, 0], brecv.at[b, 0], device_id=at(-1, 0), device_id_type=MESH),
            pltpu.make_async_remote_copy(own_s.at[b], north_s.at[b], bsend.at[b, 1], brecv.at[b, 1], device_id=at(1, 0), device_id_type=MESH),
        ]
        for cp in pair:
            cp.start()
        sends.append(pair)

    loads[6].wait()
    for cp in metas:
        cp.wait()
    build_onehot(1, meta_n)
    build_onehot(2, meta_d)

    for b in range(NB):
        for cp in sends[b]:
            cp.wait()
        for q in range(3):
            part = slice(q * 192, (q + 1) * 192)
            if b == 0:
                total = back_s[part, :].astype(F32)
                for k in range(NB):
                    total += jnp.dot(onehot_s[k, part, :], own_s[k], preferred_element_type=F32)
            else:
                total = sum_s[part, :]
            total += jnp.dot(onehot_s[2 + b, part, :], north_s[b], preferred_element_type=F32)
            total += jnp.dot(onehot_s[4 + b, part, :], south_s[b], preferred_element_type=F32)
            if b == 0:
                sum_s[part, :] = total
            else:
                st_s[0, part, :] = total.astype(BF16)

    for cp in loads[7:]:
        cp.wait()

    has_top = jnp.where(lat > 0, 1.0, 0.0).astype(F32)
    has_bot = jnp.where(lat < nlat - 1, 1.0, 0.0).astype(F32)

    for l in range(LAYERS):
        st = st_s.at[l]
        edge_l[l] = jnp.dot(pick_ls[...], st[...], preferred_element_type=F32).astype(BF16)
        edge_r[l] = jnp.dot(pick_rs[...], st[...], preferred_element_type=F32).astype(BF16)
        moves = [
            (st.at[pl.ds(496, 80)], top_s.at[l], (1, 0)),
            (st.at[pl.ds(0, 80)], bot_s.at[l], (-1, 0)),
            (edge_r.at[l, pl.ds(16, 80)], strip_l.at[l, pl.ds(16, 80)], (0, 1)),
            (edge_l.at[l, pl.ds(16, 80)], strip_r.at[l, pl.ds(16, 80)], (0, -1)),
            (edge_r.at[l, pl.ds(0, 16)], strip_l.at[l, pl.ds(0, 16)], (1, 1)),
            (edge_r.at[l, pl.ds(96, 16)], strip_l.at[l, pl.ds(96, 16)], (-1, 1)),
            (edge_l.at[l, pl.ds(0, 16)], strip_r.at[l, pl.ds(0, 16)], (1, -1)),
            (edge_l.at[l, pl.ds(96, 16)], strip_r.at[l, pl.ds(96, 16)], (-1, -1)),
        ]
        copies = [
            pltpu.make_async_remote_copy(src, dst, hsend.at[l, n], hrecv.at[l, n], device_id=at(*d), device_id_type=MESH)
            for n, (src, dst, d) in enumerate(moves)
        ]
        for cp in copies:
            cp.start()
        for c in range(2):
            lanes = slice(c * 128, (c + 1) * 128)
            pad_s[c, 3:27, 8:32, :] = st[:, lanes].astype(F32).reshape(T, T, 128)
        for cp in copies:
            cp.wait()
        left = jnp.dot(spread_ls[...], strip_l[l], preferred_element_type=F32).reshape(30, 8, C)
        right = jnp.dot(spread_rs[...], strip_r[l], preferred_element_type=F32).reshape(30, 8, C)
        upper = top_s[l].astype(F32)[8:80].reshape(3, T, C) * has_top
        lower = bot_s[l].astype(F32)[0:72].reshape(3, T, C) * has_bot
        for c in range(2):
            lanes = slice(c * 128, (c + 1) * 128)
            for side, lo in ((left, 0), (right, 32)):
                pad_s[c, 0:3, lo:lo + 8, :] = side[0:3, :, lanes] * has_top
                pad_s[c, 3:27, lo:lo + 8, :] = side[3:27, :, lanes]
                pad_s[c, 27:30, lo:lo + 8, :] = side[27:30, :, lanes] * has_bot
            pad_s[c, 0:3, 8:32, :] = upper[:, :, lanes]
            pad_s[c, 27:30, 8:32, :] = lower[:, :, lanes]

        def mix_rows(h0, c, l=l):
            lanes = slice(c * 128, (c + 1) * 128)
            acc = [None] * 8
            for e in range(KS):
                wt = [dep_s[a, e, l:l + 1, lanes] for a in range(KS)]
                for r in range(14):
                    line = pad_s[c, h0 + r, 5 + e:29 + e, :]
                    for a in range(KS):
                        o = r - a
                        if 0 <= o < 8:
                            term = line * wt[a]
                            acc[o] = term if acc[o] is None else acc[o] + term
            for o in range(8):
                mix_s[c, h0 + o] = acc[o]

        for c in range(2):
            def mix_step(g, _, c=c):
                mix_rows(g * 8, c)
                return 0

            lax.fori_loop(0, 3, mix_step, 0)

        for g in range(2):
            part = slice(g * 288, (g + 1) * 288)
            m0 = mix_s[0, g * 12:(g + 1) * 12].reshape(288, 128)
            m1 = mix_s[1, g * 12:(g + 1) * 12].reshape(288, 128)
            mean = jnp.sum(m0 + m1, axis=-1, keepdims=True) * (1.0 / C)
            c0, c1 = m0 - mean, m1 - mean
            var = jnp.sum(c0 * c0 + c1 * c1, axis=-1, keepdims=True) * (1.0 / C)
            inv = lax.rsqrt(var + 1e-6)
            normed = jnp.concatenate(
                [(c0 * inv * gain_s[l:l + 1, 0:128]).astype(BF16), (c1 * inv * gain_s[l:l + 1, 128:256]).astype(BF16)], axis=1
            )
            new = st[part, :].astype(F32)
            for q in range(4):
                hq = slice(q * 256, (q + 1) * 256)
                hid = gelu(jnp.dot(normed, up_s[l, :, hq], preferred_element_type=F32)).astype(BF16)
                new += jnp.dot(hid, dn_s[l, hq, :], preferred_element_type=F32)
            if l == LAYERS - 1:
                out[part, :] = new.astype(BF16)
            else:
                st_s[l + 1, part, :] = new.astype(BF16)


def solution(mesh):
    nlat, nlon = mesh.shape["lat"], mesh.shape["lon"]

    def per_device(swath, wconv, bias, band, roff, coff, roww, colw, back, depth, gain, up, down):
        smem = pl.BlockSpec(memory_space=pltpu.SMEM)
        vmem = pl.BlockSpec(memory_space=pltpu.VMEM)
        hbm = pl.BlockSpec(memory_space=pl.ANY)
        dma = pltpu.SemaphoreType.DMA
        result = pl.pallas_call(
            functools.partial(body, nlat, nlon),
            out_shape=pltpu.VMEM((CELLS, C), BF16),
            in_specs=[smem] * 3 + [hbm] * 14,
            out_specs=vmem,
            scratch_shapes=[
                pltpu.VMEM((NB, IB, IB, C), BF16),
                pltpu.VMEM((3, 3 * C, C), BF16),
                pltpu.VMEM((LAYERS, C, HID), BF16),
                pltpu.VMEM((LAYERS, HID, C), BF16),
                pltpu.VMEM((SLOTS, 2, 8, 72, 128), F32),
                pltpu.VMEM((33, 2, OB, 3 * C), BF16),
                pltpu.VMEM((OB * OB, C), BF16),
                pltpu.VMEM((NB, RB * RB, OB * OB), BF16),
                pltpu.VMEM((NB, RB * RB, C), BF16),
                pltpu.VMEM((NB, RB * RB, C), BF16),
                pltpu.VMEM((NB, RB * RB, C), BF16),
                pltpu.VMEM((3, 8, C), jnp.int32),
                pltpu.VMEM((8, C), jnp.int32),
                pltpu.VMEM((8, C), jnp.int32),
                pltpu.VMEM((3 * NB, CELLS, RB * RB), BF16),
                pltpu.VMEM((CELLS, C), jnp.int32),
                pltpu.VMEM((CELLS, C), F32),
                pltpu.VMEM((LAYERS, CELLS, C), BF16),
                pltpu.VMEM((2, 30, 40, 128), F32),
                pltpu.VMEM((2, T, T, 128), F32),
                pltpu.VMEM((LAYERS, STRIP, C), BF16),
                pltpu.VMEM((LAYERS, STRIP, C), BF16),
                pltpu.VMEM((LAYERS, STRIP, C), BF16),
                pltpu.VMEM((LAYERS, STRIP, C), BF16),
                pltpu.VMEM((LAYERS, 80, C), BF16),
                pltpu.VMEM((LAYERS, 80, C), BF16),
                pltpu.VMEM((NB, RB, OB), BF16),
                pltpu.VMEM((NB, RB, OB), BF16),
                pltpu.VMEM((1, C), F32),
                pltpu.VMEM((CELLS, C), BF16),
                pltpu.VMEM((STRIP, CELLS), BF16),
                pltpu.VMEM((STRIP, CELLS), BF16),
                pltpu.VMEM((240, STRIP), BF16),
                pltpu.VMEM((240, STRIP), BF16),
                pltpu.VMEM((KS, KS, LAYERS, C), F32),
                pltpu.VMEM((LAYERS, C), F32),
                dma((15,)),
                dma((NB, 2)),
                dma((NB, 2)),
                dma((2,)),
                dma((2,)),
                dma((LAYERS, 8)),
                dma((LAYERS, 8)),
            ],
            compiler_params=pltpu.CompilerParams(
                collective_id=0, has_side_effects=True, vmem_limit_bytes=56 * 1024 * 1024
            ),
        )(
            band.reshape(NB), roff, coff, swath, wconv.reshape(3, 3 * C, C), bias.reshape(1, C), roww, colw,
            back.reshape(CELLS, C), jnp.transpose(depth, (1, 2, 0, 3)), gain, up, down,
            jnp.asarray(pick_matrix(0), BF16), jnp.asarray(pick_matrix(T - HALO), BF16),
            jnp.asarray(spread_matrix(5), BF16), jnp.asarray(spread_matrix(0), BF16),
        )
        return result.reshape(T, T, C)

    split = P(("lat", "lon"))
    in_specs = (split, P(), P(), split, split, split, split, split, P("lat", "lon"), P(), P(), P(), P())
    return jax.shard_map(
        per_device, mesh=mesh, in_specs=in_specs, out_specs=P("lat", "lon", None), check_vma=False
    )
```

```python
import functools

import jax
import jax.numpy as jnp
import numpy as np
from jax import lax
from jax.experimental import pallas as pl
from jax.experimental.pallas import tpu as pltpu
from jax.sharding import PartitionSpec as P

KS = 7
HALO = 3
LAYERS = 2
NB = 2
OB = 32
IB = 64
RB = 16
T = 24
CELLS = T * T
C = 256
HID = 1024
SLOTS = 2
STRIP = 112
F32 = jnp.float32
BF16 = jnp.bfloat16
MESH = pl.DeviceIdType.MESH
DIAGS = ((1, 0), (-1, 0), (0, 1), (0, -1), (1, 1), (-1, 1), (1, -1), (-1, -1))


def strip_source(first_col):
    cells = np.full((STRIP,), -1)
    for k in range(9):
        cells[k] = (T - HALO + k // 3) * T + first_col + k % 3
        cells[96 + k] = (k // 3) * T + first_col + k % 3
    for k in range(3 * T):
        cells[16 + k] = (k // 3) * T + first_col + k % 3
    return cells


def pick_matrix(first_col):
    return (strip_source(first_col)[:, None] == np.arange(CELLS)[None, :]).astype(np.float32)


def spread_matrix(first):
    out = np.zeros((30 * 8, STRIP), np.float32)
    for y in range(30):
        base = y * 3 if y < 3 else (16 + (y - 3) * 3 if y < 27 else 96 + (y - 27) * 3)
        for t in range(3):
            out[y * 8 + first + t, base + t] = 1
    return out


def gelu(x):
    inner = x * (0.7978845608028654 + 0.035677408136300125 * (x * x))
    half = 0.5 * x
    return half + half * jnp.tanh(inner)


def body(
    nlat, nlon,
    band, roff, coff, swath, wconv, bias, roww, colw, back, depth, gain, up, down,
    pick_l, pick_r, spread_l, spread_r,
    out,
    x_s, w_s, up_s, dn_s, t_s, x3_s, feat_s, kron_s, own_s, north_s, south_s,
    meta_s, meta_n, meta_d, onehot_s, acc_s, sum_s, st_s, pad_s, mix_s,
    edge_l, edge_r, strip_l, strip_r, top_s, bot_s,
    roww_s, colw_s, bias_s, back_s, pick_ls, pick_rs, spread_ls, spread_rs, dep_s, gain_s, raw_s, west_s, east_s, rows_s,
    load_sem, bsend, brecv, msend, mrecv, hsend, hrecv,
):
    lat, lon = lax.axis_index("lat"), lax.axis_index("lon")

    def at(dlat, dlon):
        return (lax.rem(lat + dlat + nlat, nlat), lax.rem(lon + dlon + nlon, nlon))

    barrier = pltpu.get_barrier_semaphore()
    for d in DIAGS:
        pl.semaphore_signal(barrier, inc=1, device_id=at(*d), device_id_type=MESH)

    loads = [
        pltpu.make_async_copy(src, dst, load_sem.at[n])
        for n, (src, dst) in enumerate((
            (roww, roww_s), (colw, colw_s), (swath.at[0], x_s.at[0]), (bias, bias_s), (wconv, w_s), (swath.at[1], x_s.at[1]),
            (back, back_s), (pick_l, pick_ls), (pick_r, pick_rs), (spread_l, spread_ls), (spread_r, spread_rs),
            (depth, raw_s), (gain, gain_s), (up, up_s), (down, dn_s),
        ))
    ]
    for cp in loads:
        cp.start()

    row8 = lax.broadcasted_iota(jnp.int32, (8, C), 0)

    def codes(target):
        c0 = jnp.where(band[0] == target, roff[0] * 64 + coff[0], -4096)
        c1 = jnp.where(band[1] == target, roff[1] * 64 + coff[1], -4096)
        return jnp.where(row8 == 0, c0, jnp.where(row8 == 1, c1, -4096))

    meta_s[0] = codes(lat)
    meta_s[1] = codes(lat - 1)
    meta_s[2] = codes(lat + 1)

    cell = lax.broadcasted_iota(jnp.int32, (CELLS, C), 0)
    pos = lax.broadcasted_iota(jnp.int32, (CELLS, C), 1)
    h = (cell * 2731) >> 16
    w = cell - h * T
    diff = (h - (pos >> 4)) * 64 + (w - (pos & 15))
    acc_s[...] = diff

    def build_onehot(slot, meta_ref):
        for s in range(NB):
            code = meta_ref[s:s + 1, :]
            onehot_s[2 * slot + s] = jnp.where(acc_s[...] == code, 1.0, 0.0).astype(BF16)

    build_onehot(0, meta_s.at[0])

    m_i = lax.broadcasted_iota(jnp.int32, (RB * RB, RB), 0)
    r_i = lax.broadcasted_iota(jnp.int32, (RB * RB, RB), 1)
    exp_r = jnp.where((m_i >> 4) == r_i, 1.0, 0.0).astype(BF16)
    exp_u = jnp.where((m_i & 15) == r_i, 1.0, 0.0).astype(BF16)
    k_i = lax.broadcasted_iota(jnp.int32, (OB, OB * OB), 1)
    i_i = lax.broadcasted_iota(jnp.int32, (OB, OB * OB), 0)
    exp_i = jnp.where((k_i >> 5) == i_i, 1.0, 0.0).astype(BF16)
    exp_j = jnp.where((k_i & 31) == i_i, 1.0, 0.0).astype(BF16)
    loads[0].wait()
    loads[1].wait()
    for b in range(NB):
        rows = jnp.dot(exp_r, roww_s[b], preferred_element_type=F32).astype(BF16)
        cols = jnp.dot(exp_u, colw_s[b], preferred_element_type=F32).astype(BF16)
        for q in range(4):
            part = slice(q * 256, (q + 1) * 256)
            left = jnp.dot(rows, exp_i[:, part], preferred_element_type=F32)
            right = jnp.dot(cols, exp_j[:, part], preferred_element_type=F32)
            kron_s[b, :, part] = (left * right).astype(BF16)

    t_s[:, :, :, 0:8, :] = jnp.zeros((SLOTS, 2, 8, 8, 128), F32)
    x3_s[0, 0] = jnp.zeros((OB, 3 * C), BF16)

    sends = []
    for b in range(NB):
        loads[2 if b == 0 else 5].wait()
        if b == 0:
            loads[3].wait()
            loads[4].wait()

        def spread_rows(g, b=b):
            slot = g % SLOTS
            for k in range(8):
                for c in range(2):
                    t_s[slot, c, k, 8:72, :] = x_s[b, g * 8 + k, :, c * 128:(c + 1) * 128].astype(F32)
            for k in range(8):
                hi, lo = (k + 1) // 2, (k + 1) % 2
                for e in range(3):
                    for c in range(2):
                        piece = t_s[slot, c, k, pl.ds(7 + e, OB, stride=2), :].astype(BF16)
                        x3_s[g * 4 + hi, lo, :, e * C + c * 128:e * C + (c + 1) * 128] = piece

        def conv_rows(g):
            i0 = g * 8
            total = jnp.dot(x3_s[i0:i0 + 8, 0].reshape(256, 3 * C), w_s[0], preferred_element_type=F32)
            total += jnp.dot(x3_s[i0:i0 + 8, 1].reshape(256, 3 * C), w_s[1], preferred_element_type=F32)
            total += jnp.dot(x3_s[i0 + 1:i0 + 9, 0].reshape(256, 3 * C), w_s[2], preferred_element_type=F32)
            feat_s[g * 256:(g + 1) * 256, :] = gelu(total + bias_s[...]).astype(BF16)

        spread_rows(0)
        spread_rows(1)
        for g in range(4):
            if g < 3:
                spread_rows(2 * g + 2)
                spread_rows(2 * g + 3)
            conv_rows(g)
        own_s[b] = jnp.dot(kron_s[b], feat_s[...], preferred_element_type=F32).astype(BF16)
        if b == 0:
            pl.semaphore_wait(barrier, len(DIAGS))
            metas = [
                pltpu.make_async_remote_copy(meta_s.at[1], meta_d, msend.at[0], mrecv.at[0], device_id=at(-1, 0), device_id_type=MESH),
                pltpu.make_async_remote_copy(meta_s.at[2], meta_n, msend.at[1], mrecv.at[1], device_id=at(1, 0), device_id_type=MESH),
            ]
            for cp in metas:
                cp.start()
        pair = [
            pltpu.make_async_remote_copy(own_s.at[b], south_s.at[b], bsend.at[b, 0], brecv.at[b, 0], device_id=at(-1, 0), device_id_type=MESH),
            pltpu.make_async_remote_copy(own_s.at[b], north_s.at[b], bsend.at[b, 1], brecv.at[b, 1], device_id=at(1, 0), device_id_type=MESH),
        ]
        for cp in pair:
            cp.start()
        sends.append(pair)

    loads[6].wait()
    for cp in loads[7:]:
        cp.wait()
    for ref in (pad_s, west_s, east_s, rows_s):
        ref[...] = jnp.zeros(ref.shape, F32)
    for l in range(LAYERS):
        for c in range(2):
            for e in range(KS):
                for a in range(KS):
                    dep_s[2 * l + c, a * KS + e] = jnp.broadcast_to(raw_s[a, e, l:l + 1, c * 128:(c + 1) * 128], (8, 128))
    for cp in metas:
        cp.wait()
    build_onehot(1, meta_n)
    build_onehot(2, meta_d)

    for b in range(NB):
        for cp in sends[b]:
            cp.wait()
        for q in range(3):
            part = slice(q * 192, (q + 1) * 192)
            if b == 0:
                total = back_s[part, :].astype(F32)
                for k in range(NB):
                    total += jnp.dot(onehot_s[k, part, :], own_s[k], preferred_element_type=F32)
            else:
                total = sum_s[part, :]
            total += jnp.dot(onehot_s[2 + b, part, :], north_s[b], preferred_element_type=F32)
            total += jnp.dot(onehot_s[4 + b, part, :], south_s[b], preferred_element_type=F32)
            if b == 0:
                sum_s[part, :] = total
            else:
                st_s[0, part, :] = total.astype(BF16)

    has_top = jnp.where(lat > 0, 1.0, 0.0).astype(F32)
    has_bot = jnp.where(lat < nlat - 1, 1.0, 0.0).astype(F32)

    for l in range(LAYERS):
        st = st_s.at[l]
        edge_l[l] = jnp.dot(pick_ls[...], st[...], preferred_element_type=F32).astype(BF16)
        edge_r[l] = jnp.dot(pick_rs[...], st[...], preferred_element_type=F32).astype(BF16)
        moves = [
            (st.at[pl.ds(496, 80)], top_s.at[l], (1, 0)),
            (st.at[pl.ds(0, 80)], bot_s.at[l], (-1, 0)),
            (edge_r.at[l, pl.ds(16, 80)], strip_l.at[l, pl.ds(16, 80)], (0, 1)),
            (edge_l.at[l, pl.ds(16, 80)], strip_r.at[l, pl.ds(16, 80)], (0, -1)),
            (edge_r.at[l, pl.ds(0, 16)], strip_l.at[l, pl.ds(0, 16)], (1, 1)),
            (edge_r.at[l, pl.ds(96, 16)], strip_l.at[l, pl.ds(96, 16)], (-1, 1)),
            (edge_l.at[l, pl.ds(0, 16)], strip_r.at[l, pl.ds(0, 16)], (1, -1)),
            (edge_l.at[l, pl.ds(96, 16)], strip_r.at[l, pl.ds(96, 16)], (-1, -1)),
        ]
        copies = [
            pltpu.make_async_remote_copy(src, dst, hsend.at[l, n], hrecv.at[l, n], device_id=at(*d), device_id_type=MESH)
            for n, (src, dst, d) in enumerate(moves)
        ]
        for cp in copies:
            cp.start()
        for c in range(2):
            pad_s[c, 3:27, 8:32, :] = st[:, c * 128:(c + 1) * 128].astype(F32).reshape(T, T, 128)

        def weights(c, e, l=l):
            return [dep_s[2 * l + c, a * KS + e] for a in range(KS)]

        def mix_own(g, _):
            c, h0 = g // 3, (g % 3) * 8
            acc = [None] * 8
            for e in range(KS):
                wt = weights(c, e)
                for r in range(14):
                    line = pad_s[c, h0 + r, 5 + e:29 + e, :].reshape(3, 8, 128)
                    for a in range(KS):
                        o = r - a
                        if 0 <= o < 8:
                            term = line * wt[a]
                            acc[o] = term if acc[o] is None else acc[o] + term
            for o in range(8):
                mix_s[c, h0 + o] = acc[o].reshape(T, 128)
            return 0

        lax.fori_loop(0, 6, mix_own, 0)

        for cp in copies[2:]:
            cp.wait()
        for ref, place, strip in ((west_s, spread_ls, strip_l), (east_s, spread_rs, strip_r)):
            side = jnp.dot(place[...], strip[l], preferred_element_type=F32).reshape(30, 8, C)
            lo = 0 if ref is west_s else 8
            for c in range(2):
                lanes = slice(c * 128, (c + 1) * 128)
                ref[c, 0:3, lo:lo + 8, :] = side[0:3, :, lanes] * has_top
                ref[c, 3:27, lo:lo + 8, :] = side[3:27, :, lanes]
                ref[c, 27:30, lo:lo + 8, :] = side[27:30, :, lanes] * has_bot

        def mix_sides(g, _):
            c, h0 = g // 3, (g % 3) * 8
            for ref, shifts, first, col in ((west_s, (0, 1, 2), 5, 0), (east_s, (4, 5, 6), -3, 16)):
                acc = [mix_s[c, h0 + o, col:col + 8, :] for o in range(8)]
                for e in shifts:
                    wt = weights(c, e)
                    for r in range(14):
                        line = ref[c, h0 + r, first + e:first + e + 8, :]
                        for a in range(KS):
                            if 0 <= r - a < 8:
                                acc[r - a] += line * wt[a]
                for o in range(8):
                    mix_s[c, h0 + o, col:col + 8, :] = acc[o]
            return 0

        lax.fori_loop(0, 6, mix_sides, 0)

        for cp in copies[:2]:
            cp.wait()
        upper = top_s[l].astype(F32)[8:80].reshape(3, T, C) * has_top
        lower = bot_s[l].astype(F32)[0:72].reshape(3, T, C) * has_bot
        for c in range(2):
            lanes = slice(c * 128, (c + 1) * 128)
            rows_s[0, c, :, 8:32, :] = upper[:, :, lanes]
            rows_s[1, c, :, 8:32, :] = lower[:, :, lanes]

        def mix_ends(c, _):
            for side, h0 in ((0, 0), (1, T - HALO)):
                acc = [mix_s[c, h0 + o].reshape(3, 8, 128) for o in range(3)]
                for e in range(KS):
                    wt = weights(c, e)
                    for r in range(3):
                        line = rows_s[side, c, r, 5 + e:29 + e, :].reshape(3, 8, 128)
                        for o in range(3):
                            a = r - o if side == 0 else 6 + r - o
                            if 0 <= a < KS:
                                acc[o] += line * wt[a]
                for o in range(3):
                    mix_s[c, h0 + o] = acc[o].reshape(T, 128)
            return 0

        lax.fori_loop(0, 2, mix_ends, 0)

        for g in range(2):
            part = slice(g * 288, (g + 1) * 288)
            m0 = mix_s[0, g * 12:(g + 1) * 12].reshape(288, 128)
            m1 = mix_s[1, g * 12:(g + 1) * 12].reshape(288, 128)
            mean = jnp.sum(m0 + m1, axis=-1, keepdims=True) * (1.0 / C)
            c0, c1 = m0 - mean, m1 - mean
            var = jnp.sum(c0 * c0 + c1 * c1, axis=-1, keepdims=True) * (1.0 / C)
            inv = lax.rsqrt(var + 1e-6)
            normed = jnp.concatenate(
                [(c0 * inv * gain_s[l:l + 1, 0:128]).astype(BF16), (c1 * inv * gain_s[l:l + 1, 128:256]).astype(BF16)], axis=1
            )
            new = st[part, :].astype(F32)
            for q in range(4):
                hq = slice(q * 256, (q + 1) * 256)
                hid = gelu(jnp.dot(normed, up_s[l, :, hq], preferred_element_type=F32)).astype(BF16)
                new += jnp.dot(hid, dn_s[l, hq, :], preferred_element_type=F32)
            if l == LAYERS - 1:
                out[part, :] = new.astype(BF16)
            else:
                st_s[l + 1, part, :] = new.astype(BF16)


def solution(mesh):
    nlat, nlon = mesh.shape["lat"], mesh.shape["lon"]

    def per_device(swath, wconv, bias, band, roff, coff, roww, colw, back, depth, gain, up, down):
        smem = pl.BlockSpec(memory_space=pltpu.SMEM)
        vmem = pl.BlockSpec(memory_space=pltpu.VMEM)
        hbm = pl.BlockSpec(memory_space=pl.ANY)
        dma = pltpu.SemaphoreType.DMA
        result = pl.pallas_call(
            functools.partial(body, nlat, nlon),
            out_shape=pltpu.VMEM((CELLS, C), BF16),
            in_specs=[smem] * 3 + [hbm] * 14,
            out_specs=vmem,
            scratch_shapes=[
                pltpu.VMEM((NB, IB, IB, C), BF16),
                pltpu.VMEM((3, 3 * C, C), BF16),
                pltpu.VMEM((LAYERS, C, HID), BF16),
                pltpu.VMEM((LAYERS, HID, C), BF16),
                pltpu.VMEM((SLOTS, 2, 8, 72, 128), F32),
                pltpu.VMEM((33, 2, OB, 3 * C), BF16),
                pltpu.VMEM((OB * OB, C), BF16),
                pltpu.VMEM((NB, RB * RB, OB * OB), BF16),
                pltpu.VMEM((NB, RB * RB, C), BF16),
                pltpu.VMEM((NB, RB * RB, C), BF16),
                pltpu.VMEM((NB, RB * RB, C), BF16),
                pltpu.VMEM((3, 8, C), jnp.int32),
                pltpu.VMEM((8, C), jnp.int32),
                pltpu.VMEM((8, C), jnp.int32),
                pltpu.VMEM((3 * NB, CELLS, RB * RB), BF16),
                pltpu.VMEM((CELLS, C), jnp.int32),
                pltpu.VMEM((CELLS, C), F32),
                pltpu.VMEM((LAYERS, CELLS, C), BF16),
                pltpu.VMEM((2, 30, 40, 128), F32),
                pltpu.VMEM((2, T, T, 128), F32),
                pltpu.VMEM((LAYERS, STRIP, C), BF16),
                pltpu.VMEM((LAYERS, STRIP, C), BF16),
                pltpu.VMEM((LAYERS, STRIP, C), BF16),
                pltpu.VMEM((LAYERS, STRIP, C), BF16),
                pltpu.VMEM((LAYERS, 80, C), BF16),
                pltpu.VMEM((LAYERS, 80, C), BF16),
                pltpu.VMEM((NB, RB, OB), BF16),
                pltpu.VMEM((NB, RB, OB), BF16),
                pltpu.VMEM((1, C), F32),
                pltpu.VMEM((CELLS, C), BF16),
                pltpu.VMEM((STRIP, CELLS), BF16),
                pltpu.VMEM((STRIP, CELLS), BF16),
                pltpu.VMEM((240, STRIP), BF16),
                pltpu.VMEM((240, STRIP), BF16),
                pltpu.VMEM((2 * LAYERS, KS * KS, 8, 128), F32),
                pltpu.VMEM((LAYERS, C), F32),
                pltpu.VMEM((KS, KS, LAYERS, C), F32),
                pltpu.VMEM((2, 30, 16, 128), F32),
                pltpu.VMEM((2, 30, 16, 128), F32),
                pltpu.VMEM((2, 2, 3, 40, 128), F32),
                dma((15,)),
                dma((NB, 2)),
                dma((NB, 2)),
                dma((2,)),
                dma((2,)),
                dma((LAYERS, 8)),
                dma((LAYERS, 8)),
            ],
            compiler_params=pltpu.CompilerParams(
                collective_id=0, has_side_effects=True, vmem_limit_bytes=56 * 1024 * 1024
            ),
        )(
            band.reshape(NB), roff, coff, swath, wconv.reshape(3, 3 * C, C), bias.reshape(1, C), roww, colw,
            back.reshape(CELLS, C), jnp.transpose(depth, (1, 2, 0, 3)), gain, up, down,
            jnp.asarray(pick_matrix(0), BF16), jnp.asarray(pick_matrix(T - HALO), BF16),
            jnp.asarray(spread_matrix(5), BF16), jnp.asarray(spread_matrix(0), BF16),
        )
        return result.reshape(T, T, C)

    split = P(("lat", "lon"))
    in_specs = (split, P(), P(), split, split, split, split, split, P("lat", "lon"), P(), P(), P(), P())
    return jax.shard_map(
        per_device, mesh=mesh, in_specs=in_specs, out_specs=P("lat", "lon", None), check_vma=False
    )
```

```python
import functools

import jax
import jax.numpy as jnp
import numpy as np
from jax import lax
from jax.experimental import pallas as pl
from jax.experimental.pallas import tpu as pltpu
from jax.sharding import PartitionSpec as P

KS = 7
HALO = 3
LAYERS = 2
NB = 2
OB = 32
IB = 64
RB = 16
T = 24
CELLS = T * T
C = 256
HID = 1024
SLOTS = 2
STRIP = 112
F32 = jnp.float32
BF16 = jnp.bfloat16
MESH = pl.DeviceIdType.MESH
DIAGS = ((1, 0), (-1, 0), (0, 1), (0, -1), (1, 1), (-1, 1), (1, -1), (-1, -1))


def strip_source(first_col):
    cells = np.full((STRIP,), -1)
    for k in range(9):
        cells[k] = (T - HALO + k // 3) * T + first_col + k % 3
        cells[96 + k] = (k // 3) * T + first_col + k % 3
    for k in range(3 * T):
        cells[16 + k] = (k // 3) * T + first_col + k % 3
    return cells


def pick_matrix(first_col):
    return (strip_source(first_col)[:, None] == np.arange(CELLS)[None, :]).astype(np.float32)


def spread_matrix(first):
    out = np.zeros((30 * 8, STRIP), np.float32)
    for y in range(30):
        base = y * 3 if y < 3 else (16 + (y - 3) * 3 if y < 27 else 96 + (y - 27) * 3)
        for t in range(3):
            out[y * 8 + first + t, base + t] = 1
    return out


def gelu(x):
    inner = x * (0.7978845608028654 + 0.035677408136300125 * (x * x))
    half = 0.5 * x
    return half + half * jnp.tanh(inner)


def body(
    nlat, nlon,
    band, roff, coff, swath, wconv, bias, roww, colw, back, depth, gain, up, down,
    pick_l, pick_r, spread_l, spread_r,
    out,
    x_s, w_s, up_s, dn_s, t_s, x3_s, feat_s, kron_s, own_s, north_s, south_s,
    meta_s, meta_n, meta_d, onehot_s, acc_s, sum_s, st_s, pad_s, mix_s,
    edge_l, edge_r, strip_l, strip_r, top_s, bot_s,
    roww_s, colw_s, bias_s, back_s, pick_ls, pick_rs, spread_ls, spread_rs, dep_s, gain_s, raw_s, west_s, east_s, rows_s,
    load_sem, bsend, brecv, msend, mrecv, hsend, hrecv,
):
    lat, lon = lax.axis_index("lat"), lax.axis_index("lon")

    def at(dlat, dlon):
        return (lax.rem(lat + dlat + nlat, nlat), lax.rem(lon + dlon + nlon, nlon))

    def where_band(step, action):
        if step == 0:
            action()
        else:
            pl.when(lat > 0 if step < 0 else lat < nlat - 1)(action)

    def start(copies):
        for step in (0, -1, 1):
            def begin(step=step):
                for d, cp in copies:
                    if d[0] == step:
                        cp.start()

            if any(d[0] == step for d, _ in copies):
                where_band(step, begin)

    def finish(copies):
        for step in (0, -1, 1):
            def end(step=step):
                for d, cp in copies:
                    if d[0] == step:
                        cp.wait_send()
                    if d[0] == -step:
                        cp.wait_recv()

            if any(d[0] in (step, -step) for d, _ in copies):
                where_band(step, end)

    barrier = pltpu.get_barrier_semaphore()
    for step in (0, -1, 1):
        def greet(step=step):
            for d in DIAGS:
                if d[0] == step:
                    pl.semaphore_signal(barrier, inc=1, device_id=at(*d), device_id_type=MESH)

        where_band(step, greet)

    @pl.when(lat == 0)
    def _():
        top_s[...] = jnp.zeros(top_s.shape, BF16)
        north_s[...] = jnp.zeros(north_s.shape, BF16)
        meta_n[...] = jnp.full(meta_n.shape, -4096, jnp.int32)
        for ref in (strip_l, strip_r):
            ref[:, 0:16, :] = jnp.zeros((LAYERS, 16, C), BF16)

    @pl.when(lat == nlat - 1)
    def _():
        bot_s[...] = jnp.zeros(bot_s.shape, BF16)
        south_s[...] = jnp.zeros(south_s.shape, BF16)
        meta_d[...] = jnp.full(meta_d.shape, -4096, jnp.int32)
        for ref in (strip_l, strip_r):
            ref[:, 96:112, :] = jnp.zeros((LAYERS, 16, C), BF16)


    loads = [
        pltpu.make_async_copy(src, dst, load_sem.at[n])
        for n, (src, dst) in enumerate((
            (roww, roww_s), (colw, colw_s), (swath.at[0], x_s.at[0]), (bias, bias_s), (wconv, w_s), (swath.at[1], x_s.at[1]),
            (back, back_s), (pick_l, pick_ls), (pick_r, pick_rs), (spread_l, spread_ls), (spread_r, spread_rs),
            (depth, raw_s), (gain, gain_s), (up, up_s), (down, dn_s),
        ))
    ]
    for cp in loads:
        cp.start()

    row8 = lax.broadcasted_iota(jnp.int32, (8, C), 0)

    def codes(target):
        c0 = jnp.where(band[0] == target, roff[0] * 64 + coff[0], -4096)
        c1 = jnp.where(band[1] == target, roff[1] * 64 + coff[1], -4096)
        return jnp.where(row8 == 0, c0, jnp.where(row8 == 1, c1, -4096))

    meta_s[0] = codes(lat)
    meta_s[1] = codes(lat - 1)
    meta_s[2] = codes(lat + 1)

    cell = lax.broadcasted_iota(jnp.int32, (CELLS, C), 0)
    pos = lax.broadcasted_iota(jnp.int32, (CELLS, C), 1)
    h = (cell * 2731) >> 16
    w = cell - h * T
    diff = (h - (pos >> 4)) * 64 + (w - (pos & 15))
    acc_s[...] = diff

    def build_onehot(slot, meta_ref):
        for s in range(NB):
            code = meta_ref[s:s + 1, :]
            onehot_s[2 * slot + s] = jnp.where(acc_s[...] == code, 1.0, 0.0).astype(BF16)

    build_onehot(0, meta_s.at[0])

    m_i = lax.broadcasted_iota(jnp.int32, (RB * RB, RB), 0)
    r_i = lax.broadcasted_iota(jnp.int32, (RB * RB, RB), 1)
    exp_r = jnp.where((m_i >> 4) == r_i, 1.0, 0.0).astype(BF16)
    exp_u = jnp.where((m_i & 15) == r_i, 1.0, 0.0).astype(BF16)
    k_i = lax.broadcasted_iota(jnp.int32, (OB, OB * OB), 1)
    i_i = lax.broadcasted_iota(jnp.int32, (OB, OB * OB), 0)
    exp_i = jnp.where((k_i >> 5) == i_i, 1.0, 0.0).astype(BF16)
    exp_j = jnp.where((k_i & 31) == i_i, 1.0, 0.0).astype(BF16)
    loads[0].wait()
    loads[1].wait()
    for b in range(NB):
        rows = jnp.dot(exp_r, roww_s[b], preferred_element_type=F32).astype(BF16)
        cols = jnp.dot(exp_u, colw_s[b], preferred_element_type=F32).astype(BF16)
        for q in range(4):
            part = slice(q * 256, (q + 1) * 256)
            left = jnp.dot(rows, exp_i[:, part], preferred_element_type=F32)
            right = jnp.dot(cols, exp_j[:, part], preferred_element_type=F32)
            kron_s[b, :, part] = (left * right).astype(BF16)

    t_s[:, :, :, 0:8, :] = jnp.zeros((SLOTS, 2, 8, 8, 128), F32)
    x3_s[0, 0] = jnp.zeros((OB, 3 * C), BF16)

    sends = []
    for b in range(NB):
        loads[2 if b == 0 else 5].wait()
        if b == 0:
            loads[3].wait()
            loads[4].wait()

        def spread_rows(g, b=b):
            slot = g % SLOTS
            for k in range(8):
                for c in range(2):
                    t_s[slot, c, k, 8:72, :] = x_s[b, g * 8 + k, :, c * 128:(c + 1) * 128].astype(F32)
            for k in range(8):
                hi, lo = (k + 1) // 2, (k + 1) % 2
                for e in range(3):
                    for c in range(2):
                        piece = t_s[slot, c, k, pl.ds(7 + e, OB, stride=2), :].astype(BF16)
                        x3_s[g * 4 + hi, lo, :, e * C + c * 128:e * C + (c + 1) * 128] = piece

        def conv_rows(g):
            i0 = g * 8
            total = jnp.dot(x3_s[i0:i0 + 8, 0].reshape(256, 3 * C), w_s[0], preferred_element_type=F32)
            total += jnp.dot(x3_s[i0:i0 + 8, 1].reshape(256, 3 * C), w_s[1], preferred_element_type=F32)
            total += jnp.dot(x3_s[i0 + 1:i0 + 9, 0].reshape(256, 3 * C), w_s[2], preferred_element_type=F32)
            feat_s[g * 256:(g + 1) * 256, :] = gelu(total + bias_s[...]).astype(BF16)

        spread_rows(0)
        spread_rows(1)
        for g in range(4):
            if g < 3:
                spread_rows(2 * g + 2)
                spread_rows(2 * g + 3)
            conv_rows(g)
        own_s[b] = jnp.dot(kron_s[b], feat_s[...], preferred_element_type=F32).astype(BF16)
        if b == 0:
            at_end = (lat == 0) | (lat == nlat - 1)
            pl.when(at_end)(lambda: pl.semaphore_wait(barrier, 5))
            pl.when(jnp.logical_not(at_end))(lambda: pl.semaphore_wait(barrier, 8))
            metas = [
                ((-1, 0), pltpu.make_async_remote_copy(meta_s.at[1], meta_d, msend.at[0], mrecv.at[0], device_id=at(-1, 0), device_id_type=MESH)),
                ((1, 0), pltpu.make_async_remote_copy(meta_s.at[2], meta_n, msend.at[1], mrecv.at[1], device_id=at(1, 0), device_id_type=MESH)),
            ]
            start(metas)
        pair = [
            ((-1, 0), pltpu.make_async_remote_copy(own_s.at[b], south_s.at[b], bsend.at[b, 0], brecv.at[b, 0], device_id=at(-1, 0), device_id_type=MESH)),
            ((1, 0), pltpu.make_async_remote_copy(own_s.at[b], north_s.at[b], bsend.at[b, 1], brecv.at[b, 1], device_id=at(1, 0), device_id_type=MESH)),
        ]
        start(pair)
        sends.append(pair)

    loads[6].wait()
    for cp in loads[7:]:
        cp.wait()
    for ref in (pad_s, west_s, east_s, rows_s):
        ref[...] = jnp.zeros(ref.shape, F32)
    for l in range(LAYERS):
        for c in range(2):
            for e in range(KS):
                for a in range(KS):
                    dep_s[2 * l + c, a * KS + e] = jnp.broadcast_to(raw_s[a, e, l:l + 1, c * 128:(c + 1) * 128], (8, 128))
    finish(metas)
    build_onehot(1, meta_n)
    build_onehot(2, meta_d)

    for b in range(NB):
        finish(sends[b])
        for q in range(3):
            part = slice(q * 192, (q + 1) * 192)
            if b == 0:
                total = back_s[part, :].astype(F32)
                for k in range(NB):
                    total += jnp.dot(onehot_s[k, part, :], own_s[k], preferred_element_type=F32)
            else:
                total = sum_s[part, :]
            total += jnp.dot(onehot_s[2 + b, part, :], north_s[b], preferred_element_type=F32)
            total += jnp.dot(onehot_s[4 + b, part, :], south_s[b], preferred_element_type=F32)
            if b == 0:
                sum_s[part, :] = total
            else:
                st_s[0, part, :] = total.astype(BF16)

    for l in range(LAYERS):
        st = st_s.at[l]
        edge_l[l] = jnp.dot(pick_ls[...], st[...], preferred_element_type=F32).astype(BF16)
        edge_r[l] = jnp.dot(pick_rs[...], st[...], preferred_element_type=F32).astype(BF16)
        moves = [
            (st.at[pl.ds(496, 80)], top_s.at[l], (1, 0)),
            (st.at[pl.ds(0, 80)], bot_s.at[l], (-1, 0)),
            (edge_r.at[l, pl.ds(16, 80)], strip_l.at[l, pl.ds(16, 80)], (0, 1)),
            (edge_l.at[l, pl.ds(16, 80)], strip_r.at[l, pl.ds(16, 80)], (0, -1)),
            (edge_r.at[l, pl.ds(0, 16)], strip_l.at[l, pl.ds(0, 16)], (1, 1)),
            (edge_r.at[l, pl.ds(96, 16)], strip_l.at[l, pl.ds(96, 16)], (-1, 1)),
            (edge_l.at[l, pl.ds(0, 16)], strip_r.at[l, pl.ds(0, 16)], (1, -1)),
            (edge_l.at[l, pl.ds(96, 16)], strip_r.at[l, pl.ds(96, 16)], (-1, -1)),
        ]
        copies = [
            (d, pltpu.make_async_remote_copy(src, dst, hsend.at[l, n], hrecv.at[l, n], device_id=at(*d), device_id_type=MESH))
            for n, (src, dst, d) in enumerate(moves)
        ]
        start(copies)
        for c in range(2):
            pad_s[c, 3:27, 8:32, :] = st[:, c * 128:(c + 1) * 128].astype(F32).reshape(T, T, 128)

        def weights(c, e, l=l):
            return [dep_s[2 * l + c, a * KS + e] for a in range(KS)]

        def mix_own(g, _):
            c, h0 = g // 3, (g % 3) * 8
            acc = [None] * 8
            for e in range(KS):
                wt = weights(c, e)
                for r in range(14):
                    line = pad_s[c, h0 + r, 5 + e:29 + e, :].reshape(3, 8, 128)
                    for a in range(KS):
                        o = r - a
                        if 0 <= o < 8:
                            term = line * wt[a]
                            acc[o] = term if acc[o] is None else acc[o] + term
            for o in range(8):
                mix_s[c, h0 + o] = acc[o].reshape(T, 128)
            return 0

        lax.fori_loop(0, 6, mix_own, 0)

        finish(copies[2:])
        for ref, place, strip in ((west_s, spread_ls, strip_l), (east_s, spread_rs, strip_r)):
            side = jnp.dot(place[...], strip[l], preferred_element_type=F32).reshape(30, 8, C)
            lo = 0 if ref is west_s else 8
            for c in range(2):
                lanes = slice(c * 128, (c + 1) * 128)
                ref[c, :, lo:lo + 8, :] = side[:, :, lanes]

        def mix_sides(g, _):
            c, h0 = g // 3, (g % 3) * 8
            for ref, shifts, first, col in ((west_s, (0, 1, 2), 5, 0), (east_s, (4, 5, 6), -3, 16)):
                acc = [mix_s[c, h0 + o, col:col + 8, :] for o in range(8)]
                for e in shifts:
                    wt = weights(c, e)
                    for r in range(14):
                        line = ref[c, h0 + r, first + e:first + e + 8, :]
                        for a in range(KS):
                            if 0 <= r - a < 8:
                                acc[r - a] += line * wt[a]
                for o in range(8):
                    mix_s[c, h0 + o, col:col + 8, :] = acc[o]
            return 0

        lax.fori_loop(0, 6, mix_sides, 0)

        finish(copies[:2])
        upper = top_s[l].astype(F32)[8:80].reshape(3, T, C)
        lower = bot_s[l].astype(F32)[0:72].reshape(3, T, C)
        for c in range(2):
            lanes = slice(c * 128, (c + 1) * 128)
            rows_s[0, c, :, 8:32, :] = upper[:, :, lanes]
            rows_s[1, c, :, 8:32, :] = lower[:, :, lanes]

        def mix_ends(c, _):
            for side, h0 in ((0, 0), (1, T - HALO)):
                acc = [mix_s[c, h0 + o].reshape(3, 8, 128) for o in range(3)]
                for e in range(KS):
                    wt = weights(c, e)
                    for r in range(3):
                        line = rows_s[side, c, r, 5 + e:29 + e, :].reshape(3, 8, 128)
                        for o in range(3):
                            a = r - o if side == 0 else 6 + r - o
                            if 0 <= a < KS:
                                acc[o] += line * wt[a]
                for o in range(3):
                    mix_s[c, h0 + o] = acc[o].reshape(T, 128)
            return 0

        lax.fori_loop(0, 2, mix_ends, 0)

        for g in range(2):
            part = slice(g * 288, (g + 1) * 288)
            m0 = mix_s[0, g * 12:(g + 1) * 12].reshape(288, 128)
            m1 = mix_s[1, g * 12:(g + 1) * 12].reshape(288, 128)
            mean = jnp.sum(m0 + m1, axis=-1, keepdims=True) * (1.0 / C)
            c0, c1 = m0 - mean, m1 - mean
            var = jnp.sum(c0 * c0 + c1 * c1, axis=-1, keepdims=True) * (1.0 / C)
            inv = lax.rsqrt(var + 1e-6)
            normed = jnp.concatenate(
                [(c0 * inv * gain_s[l:l + 1, 0:128]).astype(BF16), (c1 * inv * gain_s[l:l + 1, 128:256]).astype(BF16)], axis=1
            )
            new = st[part, :].astype(F32)
            for q in range(4):
                hq = slice(q * 256, (q + 1) * 256)
                hid = gelu(jnp.dot(normed, up_s[l, :, hq], preferred_element_type=F32)).astype(BF16)
                new += jnp.dot(hid, dn_s[l, hq, :], preferred_element_type=F32)
            if l == LAYERS - 1:
                out[part, :] = new.astype(BF16)
            else:
                st_s[l + 1, part, :] = new.astype(BF16)


def solution(mesh):
    nlat, nlon = mesh.shape["lat"], mesh.shape["lon"]

    def per_device(swath, wconv, bias, band, roff, coff, roww, colw, back, depth, gain, up, down):
        smem = pl.BlockSpec(memory_space=pltpu.SMEM)
        vmem = pl.BlockSpec(memory_space=pltpu.VMEM)
        hbm = pl.BlockSpec(memory_space=pl.ANY)
        dma = pltpu.SemaphoreType.DMA
        result = pl.pallas_call(
            functools.partial(body, nlat, nlon),
            out_shape=pltpu.VMEM((CELLS, C), BF16),
            in_specs=[smem] * 3 + [hbm] * 14,
            out_specs=vmem,
            scratch_shapes=[
                pltpu.VMEM((NB, IB, IB, C), BF16),
                pltpu.VMEM((3, 3 * C, C), BF16),
                pltpu.VMEM((LAYERS, C, HID), BF16),
                pltpu.VMEM((LAYERS, HID, C), BF16),
                pltpu.VMEM((SLOTS, 2, 8, 72, 128), F32),
                pltpu.VMEM((33, 2, OB, 3 * C), BF16),
                pltpu.VMEM((OB * OB, C), BF16),
                pltpu.VMEM((NB, RB * RB, OB * OB), BF16),
                pltpu.VMEM((NB, RB * RB, C), BF16),
                pltpu.VMEM((NB, RB * RB, C), BF16),
                pltpu.VMEM((NB, RB * RB, C), BF16),
                pltpu.VMEM((3, 8, C), jnp.int32),
                pltpu.VMEM((8, C), jnp.int32),
                pltpu.VMEM((8, C), jnp.int32),
                pltpu.VMEM((3 * NB, CELLS, RB * RB), BF16),
                pltpu.VMEM((CELLS, C), jnp.int32),
                pltpu.VMEM((CELLS, C), F32),
                pltpu.VMEM((LAYERS, CELLS, C), BF16),
                pltpu.VMEM((2, 30, 40, 128), F32),
                pltpu.VMEM((2, T, T, 128), F32),
                pltpu.VMEM((LAYERS, STRIP, C), BF16),
                pltpu.VMEM((LAYERS, STRIP, C), BF16),
                pltpu.VMEM((LAYERS, STRIP, C), BF16),
                pltpu.VMEM((LAYERS, STRIP, C), BF16),
                pltpu.VMEM((LAYERS, 80, C), BF16),
                pltpu.VMEM((LAYERS, 80, C), BF16),
                pltpu.VMEM((NB, RB, OB), BF16),
                pltpu.VMEM((NB, RB, OB), BF16),
                pltpu.VMEM((1, C), F32),
                pltpu.VMEM((CELLS, C), BF16),
                pltpu.VMEM((STRIP, CELLS), BF16),
                pltpu.VMEM((STRIP, CELLS), BF16),
                pltpu.VMEM((240, STRIP), BF16),
                pltpu.VMEM((240, STRIP), BF16),
                pltpu.VMEM((2 * LAYERS, KS * KS, 8, 128), F32),
                pltpu.VMEM((LAYERS, C), F32),
                pltpu.VMEM((KS, KS, LAYERS, C), F32),
                pltpu.VMEM((2, 30, 16, 128), F32),
                pltpu.VMEM((2, 30, 16, 128), F32),
                pltpu.VMEM((2, 2, 3, 40, 128), F32),
                dma((15,)),
                dma((NB, 2)),
                dma((NB, 2)),
                dma((2,)),
                dma((2,)),
                dma((LAYERS, 8)),
                dma((LAYERS, 8)),
            ],
            compiler_params=pltpu.CompilerParams(
                collective_id=0, has_side_effects=True, vmem_limit_bytes=56 * 1024 * 1024
            ),
        )(
            band.reshape(NB), roff, coff, swath, wconv.reshape(3, 3 * C, C), bias.reshape(1, C), roww, colw,
            back.reshape(CELLS, C), jnp.transpose(depth, (1, 2, 0, 3)), gain, up, down,
            jnp.asarray(pick_matrix(0), BF16), jnp.asarray(pick_matrix(T - HALO), BF16),
            jnp.asarray(spread_matrix(5), BF16), jnp.asarray(spread_matrix(0), BF16),
        )
        return result.reshape(T, T, C)

    split = P(("lat", "lon"))
    in_specs = (split, P(), P(), split, split, split, split, split, P("lat", "lon"), P(), P(), P(), P())
    return jax.shard_map(
        per_device, mesh=mesh, in_specs=in_specs, out_specs=P("lat", "lon", None), check_vma=False
    )
```

```python
import functools

import jax
import jax.numpy as jnp
import numpy as np
from jax import lax
from jax.experimental import pallas as pl
from jax.experimental.pallas import tpu as pltpu
from jax.sharding import PartitionSpec as P

KS = 7
HALO = 3
LAYERS = 2
NB = 2
OB = 32
IB = 64
RB = 16
T = 24
CELLS = T * T
C = 256
HID = 1024
SLOTS = 2
STRIP = 112
F32 = jnp.float32
BF16 = jnp.bfloat16
MESH = pl.DeviceIdType.MESH
DIAGS = ((1, 0), (-1, 0), (0, 1), (0, -1), (1, 1), (-1, 1), (1, -1), (-1, -1))


def strip_source(first_col):
    cells = np.full((STRIP,), -1)
    for k in range(9):
        cells[k] = (T - HALO + k // 3) * T + first_col + k % 3
        cells[96 + k] = (k // 3) * T + first_col + k % 3
    for k in range(3 * T):
        cells[16 + k] = (k // 3) * T + first_col + k % 3
    return cells


def pick_matrix(first_col):
    return (strip_source(first_col)[:, None] == np.arange(CELLS)[None, :]).astype(np.float32)


def spread_matrix(first):
    out = np.zeros((30 * 8, STRIP), np.float32)
    for y in range(30):
        base = y * 3 if y < 3 else (16 + (y - 3) * 3 if y < 27 else 96 + (y - 27) * 3)
        for t in range(3):
            out[y * 8 + first + t, base + t] = 1
    return out


def gelu(x):
    inner = x * (0.7978845608028654 + 0.035677408136300125 * (x * x))
    half = 0.5 * x
    return half + half * jnp.tanh(inner)


def body(
    nlat, nlon,
    band, roff, coff, swath, wconv, bias, roww, colw, back, depth, gain, up, down,
    pick_l, pick_r, spread_l, spread_r,
    out,
    x_s, w_s, up_s, dn_s, t_s, x3_s, feat_s, kron_s, own_s, north_s, south_s,
    meta_s, meta_n, meta_d, onehot_s, acc_s, sum_s, st_s, pad_s, mix_s,
    edge_l, edge_r, strip_l, strip_r, top_s, bot_s,
    roww_s, colw_s, bias_s, back_s, pick_ls, pick_rs, spread_ls, spread_rs, dep_s, gain_s, raw_s, west_s, east_s, rows_s,
    load_sem, bsend, brecv, msend, mrecv, hsend, hrecv,
):
    lat, lon = lax.axis_index("lat"), lax.axis_index("lon")

    def at(dlat, dlon):
        return (lax.rem(lat + dlat + nlat, nlat), lax.rem(lon + dlon + nlon, nlon))

    def where_band(step, action):
        if step == 0:
            action()
        else:
            pl.when(lat > 0 if step < 0 else lat < nlat - 1)(action)

    def start(copies):
        for step in (-1, 1, 0):
            def begin(step=step):
                for d, cp in copies:
                    if d[0] == step:
                        cp.start()

            if any(d[0] == step for d, _ in copies):
                where_band(step, begin)

    def finish(copies):
        for step in (0, -1, 1):
            def end(step=step):
                for d, cp in copies:
                    if d[0] == step:
                        cp.wait_send()
                    if d[0] == -step:
                        cp.wait_recv()

            if any(d[0] in (step, -step) for d, _ in copies):
                where_band(step, end)

    barrier = pltpu.get_barrier_semaphore()
    for step in (0, -1, 1):
        def greet(step=step):
            for d in DIAGS:
                if d[0] == step:
                    pl.semaphore_signal(barrier, inc=1, device_id=at(*d), device_id_type=MESH)

        where_band(step, greet)

    @pl.when(lat == 0)
    def _():
        top_s[...] = jnp.zeros(top_s.shape, BF16)
        north_s[...] = jnp.zeros(north_s.shape, BF16)
        meta_n[...] = jnp.full(meta_n.shape, -4096, jnp.int32)
        for ref in (strip_l, strip_r):
            ref[:, 0:16, :] = jnp.zeros((LAYERS, 16, C), BF16)

    @pl.when(lat == nlat - 1)
    def _():
        bot_s[...] = jnp.zeros(bot_s.shape, BF16)
        south_s[...] = jnp.zeros(south_s.shape, BF16)
        meta_d[...] = jnp.full(meta_d.shape, -4096, jnp.int32)
        for ref in (strip_l, strip_r):
            ref[:, 96:112, :] = jnp.zeros((LAYERS, 16, C), BF16)


    loads = [
        pltpu.make_async_copy(src, dst, load_sem.at[n])
        for n, (src, dst) in enumerate((
            (roww, roww_s), (colw, colw_s), (swath.at[0], x_s.at[0]), (bias, bias_s), (wconv, w_s), (swath.at[1], x_s.at[1]),
            (back, back_s), (pick_l, pick_ls), (pick_r, pick_rs), (spread_l, spread_ls), (spread_r, spread_rs),
            (depth, raw_s), (gain, gain_s), (up, up_s), (down, dn_s),
        ))
    ]
    for cp in loads:
        cp.start()

    row8 = lax.broadcasted_iota(jnp.int32, (8, C), 0)

    def codes(target):
        c0 = jnp.where(band[0] == target, roff[0] * 64 + coff[0], -4096)
        c1 = jnp.where(band[1] == target, roff[1] * 64 + coff[1], -4096)
        return jnp.where(row8 == 0, c0, jnp.where(row8 == 1, c1, -4096))

    meta_s[0] = codes(lat)
    meta_s[1] = codes(lat - 1)
    meta_s[2] = codes(lat + 1)

    cell = lax.broadcasted_iota(jnp.int32, (CELLS, C), 0)
    pos = lax.broadcasted_iota(jnp.int32, (CELLS, C), 1)
    h = (cell * 2731) >> 16
    w = cell - h * T
    diff = (h - (pos >> 4)) * 64 + (w - (pos & 15))
    acc_s[...] = diff

    def build_onehot(slot, meta_ref):
        for s in range(NB):
            code = meta_ref[s:s + 1, :]
            onehot_s[2 * slot + s] = jnp.where(acc_s[...] == code, 1.0, 0.0).astype(BF16)

    build_onehot(0, meta_s.at[0])

    m_i = lax.broadcasted_iota(jnp.int32, (RB * RB, RB), 0)
    r_i = lax.broadcasted_iota(jnp.int32, (RB * RB, RB), 1)
    exp_r = jnp.where((m_i >> 4) == r_i, 1.0, 0.0).astype(BF16)
    exp_u = jnp.where((m_i & 15) == r_i, 1.0, 0.0).astype(BF16)
    k_i = lax.broadcasted_iota(jnp.int32, (OB, OB * OB), 1)
    i_i = lax.broadcasted_iota(jnp.int32, (OB, OB * OB), 0)
    exp_i = jnp.where((k_i >> 5) == i_i, 1.0, 0.0).astype(BF16)
    exp_j = jnp.where((k_i & 31) == i_i, 1.0, 0.0).astype(BF16)
    loads[0].wait()
    loads[1].wait()
    for b in range(NB):
        rows = jnp.dot(exp_r, roww_s[b], preferred_element_type=F32).astype(BF16)
        cols = jnp.dot(exp_u, colw_s[b], preferred_element_type=F32).astype(BF16)
        for q in range(4):
            part = slice(q * 256, (q + 1) * 256)
            left = jnp.dot(rows, exp_i[:, part], preferred_element_type=F32)
            right = jnp.dot(cols, exp_j[:, part], preferred_element_type=F32)
            kron_s[b, :, part] = (left * right).astype(BF16)

    t_s[:, :, :, 0:8, :] = jnp.zeros((SLOTS, 2, 8, 8, 128), F32)
    x3_s[0, 0] = jnp.zeros((OB, 3 * C), BF16)

    sends = []
    for b in range(NB):
        loads[2 if b == 0 else 5].wait()
        if b == 0:
            loads[3].wait()
            loads[4].wait()

        def spread_rows(g, b=b):
            slot = g % SLOTS
            for k in range(8):
                for c in range(2):
                    t_s[slot, c, k, 8:72, :] = x_s[b, g * 8 + k, :, c * 128:(c + 1) * 128].astype(F32)
            for k in range(8):
                hi, lo = (k + 1) // 2, (k + 1) % 2
                for e in range(3):
                    for c in range(2):
                        piece = t_s[slot, c, k, pl.ds(7 + e, OB, stride=2), :].astype(BF16)
                        x3_s[g * 4 + hi, lo, :, e * C + c * 128:e * C + (c + 1) * 128] = piece

        def conv_rows(g):
            i0 = g * 8
            total = jnp.dot(x3_s[i0:i0 + 8, 0].reshape(256, 3 * C), w_s[0], preferred_element_type=F32)
            total += jnp.dot(x3_s[i0:i0 + 8, 1].reshape(256, 3 * C), w_s[1], preferred_element_type=F32)
            total += jnp.dot(x3_s[i0 + 1:i0 + 9, 0].reshape(256, 3 * C), w_s[2], preferred_element_type=F32)
            feat_s[g * 256:(g + 1) * 256, :] = gelu(total + bias_s[...]).astype(BF16)

        spread_rows(0)
        spread_rows(1)
        for g in range(4):
            if g < 3:
                spread_rows(2 * g + 2)
                spread_rows(2 * g + 3)
            conv_rows(g)
        own_s[b] = jnp.dot(kron_s[b], feat_s[...], preferred_element_type=F32).astype(BF16)
        if b == 0:
            at_end = (lat == 0) | (lat == nlat - 1)
            pl.when(at_end)(lambda: pl.semaphore_wait(barrier, 5))
            pl.when(jnp.logical_not(at_end))(lambda: pl.semaphore_wait(barrier, 8))
            metas = [
                ((-1, 0), pltpu.make_async_remote_copy(meta_s.at[1], meta_d, msend.at[0], mrecv.at[0], device_id=at(-1, 0), device_id_type=MESH)),
                ((1, 0), pltpu.make_async_remote_copy(meta_s.at[2], meta_n, msend.at[1], mrecv.at[1], device_id=at(1, 0), device_id_type=MESH)),
            ]
            start(metas)
        pair = [
            ((-1, 0), pltpu.make_async_remote_copy(own_s.at[b], south_s.at[b], bsend.at[b, 0], brecv.at[b, 0], device_id=at(-1, 0), device_id_type=MESH)),
            ((1, 0), pltpu.make_async_remote_copy(own_s.at[b], north_s.at[b], bsend.at[b, 1], brecv.at[b, 1], device_id=at(1, 0), device_id_type=MESH)),
        ]
        start(pair)
        sends.append(pair)

    loads[6].wait()
    for cp in loads[7:]:
        cp.wait()
    for ref in (pad_s, west_s, east_s, rows_s):
        ref[...] = jnp.zeros(ref.shape, F32)
    for l in range(LAYERS):
        for c in range(2):
            for e in range(KS):
                for a in range(KS):
                    dep_s[2 * l + c, a * KS + e] = jnp.broadcast_to(raw_s[a, e, l:l + 1, c * 128:(c + 1) * 128], (8, 128))
    finish(metas)
    build_onehot(1, meta_n)
    build_onehot(2, meta_d)

    for b in range(NB):
        finish(sends[b])
        for q in range(3):
            part = slice(q * 192, (q + 1) * 192)
            if b == 0:
                total = back_s[part, :].astype(F32)
                for k in range(NB):
                    total += jnp.dot(onehot_s[k, part, :], own_s[k], preferred_element_type=F32)
            else:
                total = sum_s[part, :]
            total += jnp.dot(onehot_s[2 + b, part, :], north_s[b], preferred_element_type=F32)
            total += jnp.dot(onehot_s[4 + b, part, :], south_s[b], preferred_element_type=F32)
            if b == 0:
                sum_s[part, :] = total
            else:
                st_s[0, part, :] = total.astype(BF16)

    def halo_copies(l):
        st = st_s.at[l]
        moves = [
            (st.at[pl.ds(496, 80)], top_s.at[l], (1, 0)),
            (st.at[pl.ds(0, 80)], bot_s.at[l], (-1, 0)),
            (edge_r.at[l, pl.ds(16, 80)], strip_l.at[l, pl.ds(16, 80)], (0, 1)),
            (edge_l.at[l, pl.ds(16, 80)], strip_r.at[l, pl.ds(16, 80)], (0, -1)),
            (edge_r.at[l, pl.ds(0, 16)], strip_l.at[l, pl.ds(0, 16)], (1, 1)),
            (edge_r.at[l, pl.ds(96, 16)], strip_l.at[l, pl.ds(96, 16)], (-1, 1)),
            (edge_l.at[l, pl.ds(0, 16)], strip_r.at[l, pl.ds(0, 16)], (1, -1)),
            (edge_l.at[l, pl.ds(96, 16)], strip_r.at[l, pl.ds(96, 16)], (-1, -1)),
        ]
        return [
            (d, pltpu.make_async_remote_copy(src, dst, hsend.at[l, n], hrecv.at[l, n], device_id=at(*d), device_id_type=MESH))
            for n, (src, dst, d) in enumerate(moves)
        ]

    halos = [halo_copies(l) for l in range(LAYERS)]
    start(halos[0][:2])
    for l in range(LAYERS):
        st = st_s.at[l]
        copies = halos[l]
        edge_l[l] = jnp.dot(pick_ls[...], st[...], preferred_element_type=F32).astype(BF16)
        edge_r[l] = jnp.dot(pick_rs[...], st[...], preferred_element_type=F32).astype(BF16)
        start(copies[2:])
        for c in range(2):
            pad_s[c, 3:27, 8:32, :] = st[:, c * 128:(c + 1) * 128].astype(F32).reshape(T, T, 128)

        def weights(c, e, l=l):
            return [dep_s[2 * l + c, a * KS + e] for a in range(KS)]

        def mix_own(g, _):
            c, h0 = g // 6, (g % 6) * 4
            acc = [None] * 4
            for e in range(KS):
                wt = weights(c, e)
                for r in range(10):
                    line = pad_s[c, h0 + r, 5 + e:29 + e, :].reshape(3, 8, 128)
                    for a in range(KS):
                        o = r - a
                        if 0 <= o < 4:
                            term = line * wt[a]
                            acc[o] = term if acc[o] is None else acc[o] + term
            for o in range(4):
                mix_s[c, h0 + o] = acc[o].reshape(T, 128)
            return 0

        lax.fori_loop(0, 12, mix_own, 0)

        finish(copies[2:])
        for ref, place, strip in ((west_s, spread_ls, strip_l), (east_s, spread_rs, strip_r)):
            side = jnp.dot(place[...], strip[l], preferred_element_type=F32).reshape(30, 8, C)
            lo = 0 if ref is west_s else 8
            for c in range(2):
                lanes = slice(c * 128, (c + 1) * 128)
                ref[c, :, lo:lo + 8, :] = side[:, :, lanes]

        def mix_sides(g, _):
            c, h0 = g // 3, (g % 3) * 8
            for ref, shifts, first, col in ((west_s, (0, 1, 2), 5, 0), (east_s, (4, 5, 6), -3, 16)):
                acc = [mix_s[c, h0 + o, col:col + 8, :] for o in range(8)]
                for e in shifts:
                    wt = weights(c, e)
                    for r in range(14):
                        line = ref[c, h0 + r, first + e:first + e + 8, :]
                        for a in range(KS):
                            if 0 <= r - a < 8:
                                acc[r - a] += line * wt[a]
                for o in range(8):
                    mix_s[c, h0 + o, col:col + 8, :] = acc[o]
            return 0

        lax.fori_loop(0, 6, mix_sides, 0)

        finish(copies[:2])
        upper = top_s[l].astype(F32)[8:80].reshape(3, T, C)
        lower = bot_s[l].astype(F32)[0:72].reshape(3, T, C)
        for c in range(2):
            lanes = slice(c * 128, (c + 1) * 128)
            rows_s[0, c, :, 8:32, :] = upper[:, :, lanes]
            rows_s[1, c, :, 8:32, :] = lower[:, :, lanes]

        def mix_ends(c, _):
            for side, h0 in ((0, 0), (1, T - HALO)):
                acc = [mix_s[c, h0 + o].reshape(3, 8, 128) for o in range(3)]
                for e in range(KS):
                    wt = weights(c, e)
                    for r in range(3):
                        line = rows_s[side, c, r, 5 + e:29 + e, :].reshape(3, 8, 128)
                        for o in range(3):
                            a = r - o if side == 0 else 6 + r - o
                            if 0 <= a < KS:
                                acc[o] += line * wt[a]
                for o in range(3):
                    mix_s[c, h0 + o] = acc[o].reshape(T, 128)
            return 0

        lax.fori_loop(0, 2, mix_ends, 0)

        for spans in (((0, 4), (20, 24)), ((4, 20),)):
            m0, m1 = (jnp.concatenate([mix_s[c, lo:hi] for lo, hi in spans], axis=0).reshape(-1, 128) for c in range(2))
            mean = jnp.sum(m0 + m1, axis=-1, keepdims=True) * (1.0 / C)
            c0, c1 = m0 - mean, m1 - mean
            var = jnp.sum(c0 * c0 + c1 * c1, axis=-1, keepdims=True) * (1.0 / C)
            inv = lax.rsqrt(var + 1e-6)
            normed = jnp.concatenate(
                [(c0 * inv * gain_s[l:l + 1, 0:128]).astype(BF16), (c1 * inv * gain_s[l:l + 1, 128:256]).astype(BF16)], axis=1
            )
            new = jnp.concatenate([st[lo * T:hi * T, :] for lo, hi in spans], axis=0).astype(F32)
            for q in range(4):
                hq = slice(q * 256, (q + 1) * 256)
                hid = gelu(jnp.dot(normed, up_s[l, :, hq], preferred_element_type=F32)).astype(BF16)
                new += jnp.dot(hid, dn_s[l, hq, :], preferred_element_type=F32)
            target = out if l == LAYERS - 1 else st_s.at[l + 1]
            first = 0
            for lo, hi in spans:
                target[lo * T:hi * T, :] = new[first:first + (hi - lo) * T].astype(BF16)
                first += (hi - lo) * T
            if l < LAYERS - 1 and len(spans) == 2:
                start(halos[l + 1][:2])


def solution(mesh):
    nlat, nlon = mesh.shape["lat"], mesh.shape["lon"]

    def per_device(swath, wconv, bias, band, roff, coff, roww, colw, back, depth, gain, up, down):
        smem = pl.BlockSpec(memory_space=pltpu.SMEM)
        vmem = pl.BlockSpec(memory_space=pltpu.VMEM)
        hbm = pl.BlockSpec(memory_space=pl.ANY)
        dma = pltpu.SemaphoreType.DMA
        result = pl.pallas_call(
            functools.partial(body, nlat, nlon),
            out_shape=pltpu.VMEM((CELLS, C), BF16),
            in_specs=[smem] * 3 + [hbm] * 14,
            out_specs=vmem,
            scratch_shapes=[
                pltpu.VMEM((NB, IB, IB, C), BF16),
                pltpu.VMEM((3, 3 * C, C), BF16),
                pltpu.VMEM((LAYERS, C, HID), BF16),
                pltpu.VMEM((LAYERS, HID, C), BF16),
                pltpu.VMEM((SLOTS, 2, 8, 72, 128), F32),
                pltpu.VMEM((33, 2, OB, 3 * C), BF16),
                pltpu.VMEM((OB * OB, C), BF16),
                pltpu.VMEM((NB, RB * RB, OB * OB), BF16),
                pltpu.VMEM((NB, RB * RB, C), BF16),
                pltpu.VMEM((NB, RB * RB, C), BF16),
                pltpu.VMEM((NB, RB * RB, C), BF16),
                pltpu.VMEM((3, 8, C), jnp.int32),
                pltpu.VMEM((8, C), jnp.int32),
                pltpu.VMEM((8, C), jnp.int32),
                pltpu.VMEM((3 * NB, CELLS, RB * RB), BF16),
                pltpu.VMEM((CELLS, C), jnp.int32),
                pltpu.VMEM((CELLS, C), F32),
                pltpu.VMEM((LAYERS, CELLS, C), BF16),
                pltpu.VMEM((2, 30, 40, 128), F32),
                pltpu.VMEM((2, T, T, 128), F32),
                pltpu.VMEM((LAYERS, STRIP, C), BF16),
                pltpu.VMEM((LAYERS, STRIP, C), BF16),
                pltpu.VMEM((LAYERS, STRIP, C), BF16),
                pltpu.VMEM((LAYERS, STRIP, C), BF16),
                pltpu.VMEM((LAYERS, 80, C), BF16),
                pltpu.VMEM((LAYERS, 80, C), BF16),
                pltpu.VMEM((NB, RB, OB), BF16),
                pltpu.VMEM((NB, RB, OB), BF16),
                pltpu.VMEM((1, C), F32),
                pltpu.VMEM((CELLS, C), BF16),
                pltpu.VMEM((STRIP, CELLS), BF16),
                pltpu.VMEM((STRIP, CELLS), BF16),
                pltpu.VMEM((240, STRIP), BF16),
                pltpu.VMEM((240, STRIP), BF16),
                pltpu.VMEM((2 * LAYERS, KS * KS, 8, 128), F32),
                pltpu.VMEM((LAYERS, C), F32),
                pltpu.VMEM((KS, KS, LAYERS, C), F32),
                pltpu.VMEM((2, 30, 16, 128), F32),
                pltpu.VMEM((2, 30, 16, 128), F32),
                pltpu.VMEM((2, 2, 3, 40, 128), F32),
                dma((15,)),
                dma((NB, 2)),
                dma((NB, 2)),
                dma((2,)),
                dma((2,)),
                dma((LAYERS, 8)),
                dma((LAYERS, 8)),
            ],
            compiler_params=pltpu.CompilerParams(
                collective_id=0, has_side_effects=True, vmem_limit_bytes=56 * 1024 * 1024
            ),
        )(
            band.reshape(NB), roff, coff, swath, wconv.reshape(3, 3 * C, C), bias.reshape(1, C), roww, colw,
            back.reshape(CELLS, C), jnp.transpose(depth, (1, 2, 0, 3)), gain, up, down,
            jnp.asarray(pick_matrix(0), BF16), jnp.asarray(pick_matrix(T - HALO), BF16),
            jnp.asarray(spread_matrix(5), BF16), jnp.asarray(spread_matrix(0), BF16),
        )
        return result.reshape(T, T, C)

    split = P(("lat", "lon"))
    in_specs = (split, P(), P(), split, split, split, split, split, P("lat", "lon"), P(), P(), P(), P())
    return jax.shard_map(
        per_device, mesh=mesh, in_specs=in_specs, out_specs=P("lat", "lon", None), check_vma=False
    )
```
